128 devices in a mesh: clip: 8 (over y, core), sess: 16 (over z, x).
Axes of the slice: x: 4, y: 4, z: 4, core: 2. Of those that a mesh axis runs over, the one named last changes fastest.
Arguments:
- video: bfloat16 [128, 16, 2304], P('clip', 'sess'), may hold values from -6 to 6
- responses: bfloat16 [128, 16, 4096], P('clip', 'sess'), may hold values from 0 to 0.5
- assignment: int32 [128], P('clip'), may hold values from 0 to 15, as said below
- counts: int32 [16], P('sess'), may hold values from 1024 to 4096, as said below
- conv_weight: bfloat16 [64, 147], replicated, may hold values from -0.5 to 0.5
- conv_bias: float32 [64], replicated, may hold values from -3 to 3
- mix_weight: bfloat16 [64, 64], replicated, may hold values from -0.75 to 0.75
- mix_bias: float32 [64], replicated, may hold values from -3 to 3
- masks: bfloat16 [16, 4096, 576], P('sess'), may hold values from -0.25 to 0.25
- feat_w: bfloat16 [16, 4096, 64], P('sess'), may hold values from -0.75 to 0.75
- readout_bias: float32 [16, 4096], P('sess'), may hold values from -1 to 1
Outputs:
- loss: float32 [], replicated
- grad_conv_weight: float32 [64, 147], replicated
- grad_conv_bias: float32 [64], replicated
- grad_mix_weight: float32 [64, 64], replicated
- grad_mix_bias: float32 [64], replicated
- grad_masks: float32 [16, 4096, 576], P('sess', 'clip')
- grad_feat_w: float32 [16, 4096, 64], P('sess', 'clip')
- grad_readout_bias: float32 [16, 4096], P('sess', 'clip')
The draws below stay inside these ranges and needn't reach their ends.
Inputs may be any that keep to these rules, and one draw needn't show every extreme that they name: `assignment`: in every aligned block of 16 clips, each of the 16 sessions is named by exactly one clip. `counts`: some session has exactly 4096 neurons.
All inputs are finite; a program needn't handle non-finite values.
Results may differ from the reference program's by a relative error of at most 0.0085.
Values may be sent and summed in bfloat16 or wider, within the bound.
A program may use at most 192 MiB of HBM per device.

```python
import jax
import jax.numpy as jnp
from jax import lax

C = 64
N = 4096
HH = 36
WW = 64
KS = 7
KT = 3
SESS_DEV = 1
PIX = 2304
POOLED = 576
TAPS = 147
CLIP_DEV = 16
CLIPS = 128
FRAMES = 16
SESSIONS = 16


def draw_assignment(key, part):
    block_total = CLIPS // CLIP_DEV
    owner_total = SESSIONS // SESS_DEV
    owner_list = jnp.repeat(jnp.arange(owner_total, dtype=jnp.int32), CLIP_DEV // owner_total)
    block_keys = jax.random.split(jax.random.fold_in(key, 11), block_total)
    owners = jax.vmap(lambda block_key: jax.random.permutation(block_key, owner_list))(block_keys).reshape(-1)
    local_pick = jax.random.randint(jax.random.fold_in(key, 12), (CLIPS,), 0, SESS_DEV, dtype=jnp.int32)
    return (owners * SESS_DEV + local_pick).astype(jnp.int32)


def draw_counts(key, part):
    drawn = jax.random.randint(jax.random.fold_in(key, 21), (SESSIONS,), N // 4, N + 1, dtype=jnp.int32)
    fullest = jax.random.randint(jax.random.fold_in(key, 22), (), 0, SESSIONS, dtype=jnp.int32)
    return jnp.where(jnp.arange(SESSIONS, dtype=jnp.int32) == fullest, N, drawn).astype(jnp.int32)


def shard_levels(own_key, shape, cuts, low, high):
    def one(axis_at, shards_of):
        steps = jax.random.uniform(jax.random.fold_in(jax.random.fold_in(own_key, 6), axis_at), (shards_of,), jnp.float32, low / len(cuts), high / len(cuts))
        return jnp.repeat(jnp.exp(steps), shape[axis_at] // shards_of).reshape((-1,) + (1,) * (len(shape) - axis_at - 1))

    gain = one(*cuts[0])
    for cut in cuts[1:]:
        gain = gain * one(*cut)
    return gain


def normal_values(key, dims, width, limit, cuts=(), kind=jnp.bfloat16):
    array = width * jax.random.normal(key, dims, jnp.float32)
    if cuts:
        array = array * shard_levels(key, dims, cuts, -0.22, 0.18)
    return jnp.clip(array, -limit, limit).astype(kind)


def setup_inputs(seed: int = 0) -> dict:
    keys = jax.random.split(jax.random.key(seed), 12)
    return {
        "video": normal_values(keys[0], (CLIPS, FRAMES, PIX), 1.0, 6.0, ((0, 8), (1, 16))),
        "responses": jnp.clip(0.5 * jax.random.uniform(keys[1], (CLIPS, FRAMES, N), jnp.float32) ** shard_levels(keys[1], (CLIPS, FRAMES, N), ((0, 8), (1, 16)), -0.2, 0.2), 0.0, 0.5).astype(jnp.bfloat16),
        "assignment": draw_assignment(jax.random.fold_in(keys[11], 71), 0),
        "counts": draw_counts(jax.random.fold_in(keys[11], 71), 0),
        "conv_weight": normal_values(keys[4], (C, TAPS), TAPS ** -0.5, 0.5),
        "conv_bias": normal_values(keys[5], (C,), 0.5, 3.0, (), jnp.float32),
        "mix_weight": normal_values(keys[6], (C, C), C ** -0.5, 0.75),
        "mix_bias": normal_values(keys[7], (C,), 0.5, 3.0, (), jnp.float32),
        "masks": normal_values(keys[8], (SESSIONS, N, POOLED), POOLED ** -0.5, 0.25, ((0, 16),)),
        "feat_w": normal_values(keys[9], (SESSIONS, N, C), C ** -0.5, 0.75, ((0, 16),)),
        "readout_bias": jnp.clip(jax.random.uniform(keys[10], (SESSIONS, N), jnp.float32, -1.0, 1.0) * shard_levels(keys[10], (SESSIONS, N), ((0, 16),), -0.4, 0.0), -1.0, 1.0),
    }


def elu_slope(values):
    return jnp.where(values > 0, 1.0, jnp.exp(jnp.minimum(values, 0.0)))


def core_forward(video_pad, frames, conv_weight, conv_bias, mix_weight, mix_bias):
    clip_count = video_pad.shape[0]
    margin = KS // 2
    padded_grid = video_pad.reshape(clip_count, frames + 2, HH, WW)
    padded_grid = jnp.pad(padded_grid, ((0, 0), (0, 0), (margin, margin), (margin, margin)))
    tap_list = []
    for time_shift in range(KT):
        for row_shift in range(KS):
            for col_shift in range(KS):
                window = padded_grid[:, time_shift:time_shift + frames, row_shift:row_shift + HH, col_shift:col_shift + WW]
                tap_list.append(window.reshape(clip_count, frames, HH * WW))
    patches = jnp.stack(tap_list, 0)
    pre1 = jnp.einsum('ot,tkfp->kfop', conv_weight.astype(jnp.float32), patches.astype(jnp.float32)) + conv_bias[:, None]
    act1 = jax.nn.elu(pre1).astype(jnp.bfloat16)
    pre2 = jnp.einsum('oc,kfcp->kfop', mix_weight.astype(jnp.float32), act1.astype(jnp.float32)) + mix_bias[:, None]
    feats = jax.nn.elu(pre2).astype(jnp.bfloat16)
    return patches, pre1, act1, pre2, feats


def pool_map(feats):
    clip_count, frames, channels = feats.shape[0], feats.shape[1], feats.shape[2]
    blocks = feats.astype(jnp.float32).reshape(clip_count, frames, channels, HH // 2, 2, WW // 2, 2)
    return jnp.mean(blocks, axis=(4, 6)).reshape(clip_count, frames, channels, -1).astype(jnp.bfloat16)


def unpool_map(pooled_grad):
    clip_count, frames, channels = pooled_grad.shape[0], pooled_grad.shape[1], pooled_grad.shape[2]
    blocks = pooled_grad.reshape(clip_count, frames, channels, HH // 2, 1, WW // 2, 1)
    blocks = jnp.broadcast_to(blocks, (clip_count, frames, channels, HH // 2, 2, WW // 2, 2))
    return (blocks * 0.25).astype(jnp.bfloat16).reshape(clip_count, frames, channels, HH * WW)


def core_backward(feats_grad, patches, pre1, act1, pre2, mix_weight):
    pre2_grad = (feats_grad.astype(jnp.float32) * elu_slope(pre2)).astype(jnp.bfloat16)
    grad_mix = jnp.einsum('kfop,kfcp->oc', pre2_grad.astype(jnp.float32), act1.astype(jnp.float32))
    grad_mix_b = jnp.sum(pre2_grad.astype(jnp.float32), axis=(0, 1, 3))
    act1_grad = jnp.einsum('oc,kfop->kfcp', mix_weight.astype(jnp.float32), pre2_grad.astype(jnp.float32))
    pre1_grad = (act1_grad * elu_slope(pre1)).astype(jnp.bfloat16)
    grad_conv = jnp.einsum('kfop,tkfp->ot', pre1_grad.astype(jnp.float32), patches.astype(jnp.float32))
    grad_conv_b = jnp.sum(pre1_grad.astype(jnp.float32), axis=(0, 1, 3))
    return grad_conv, grad_conv_b, grad_mix, grad_mix_b


def readout(pooled_flat, target_all, mask, weight, rbias, live_count, row_start, row_count, loss_scale):
    frames = target_all.shape[0]
    channels = weight.shape[1]
    mask_rows = lax.dynamic_slice_in_dim(mask, row_start, row_count, 0)
    weight_rows = lax.dynamic_slice_in_dim(weight, row_start, row_count, 0).astype(jnp.float32)
    bias_rows = lax.dynamic_slice_in_dim(rbias, row_start, row_count, 0)
    target = lax.dynamic_slice_in_dim(target_all, row_start, row_count, 1).astype(jnp.float32).T
    projected = jnp.dot(mask_rows, pooled_flat.T, preferred_element_type=jnp.float32)
    w_tile = jnp.tile(weight_rows, (1, frames))
    drive = (projected * w_tile).reshape(row_count, frames, channels).sum(-1) + bias_rows[:, None]
    rate_pred = jax.nn.softplus(drive) + 0.1
    alive_rows = ((row_start + jnp.arange(row_count, dtype=jnp.int32)) < live_count)[:, None]
    loss_sum = jnp.sum(jnp.where(alive_rows, rate_pred - target * jnp.log(rate_pred), 0.0)) * loss_scale
    grad_drive = jnp.where(alive_rows, (1.0 - target / rate_pred) * jax.nn.sigmoid(drive), 0.0) * loss_scale
    spread = jnp.repeat(grad_drive, channels, axis=1)
    feat_grad = (spread * projected).reshape(row_count, frames, channels).sum(1)
    mixed = (spread * w_tile).astype(jnp.bfloat16)
    mask_grad = jnp.dot(mixed, pooled_flat, preferred_element_type=jnp.float32)
    pooled_grad = jnp.dot(mixed.T, mask_rows, preferred_element_type=jnp.float32)
    return loss_sum, pooled_grad, mask_grad, feat_grad, jnp.sum(grad_drive, axis=1)


def reference(video, responses, assignment, counts, conv_weight, conv_bias, mix_weight, mix_bias, masks, feat_w, readout_bias):
    loss_scale = 1.0 / (CLIPS * FRAMES)

    def one_clip(carried, inputs):
        clip_video, clip_target, session = inputs
        video_pad = jnp.pad(clip_video, ((1, 1), (0, 0)))[None]
        patches, pre1, act1, pre2, feats = core_forward(video_pad, FRAMES, conv_weight, conv_bias, mix_weight, mix_bias)
        pooled = pool_map(feats)
        pooled_flat = pooled[0].reshape(FRAMES * C, -1)
        mask = lax.dynamic_index_in_dim(masks, session, 0, keepdims=False)
        weight = lax.dynamic_index_in_dim(feat_w, session, 0, keepdims=False)
        rbias = lax.dynamic_index_in_dim(readout_bias, session, 0, keepdims=False)
        live_count = lax.dynamic_index_in_dim(counts, session, 0, keepdims=False)
        loss_sum, pooled_grad, mask_grad, feat_grad, bias_grad = readout(pooled_flat, clip_target, mask, weight, rbias, live_count, 0, N, loss_scale)
        pooled_grad = pooled_grad.astype(jnp.bfloat16).reshape(1, FRAMES, C, -1)
        feats_grad = unpool_map(pooled_grad)
        core_parts = core_backward(feats_grad, patches, pre1, act1, pre2, mix_weight)
        new_carry = (carried[0] + loss_sum,
                     carried[1] + core_parts[0], carried[2] + core_parts[1],
                     carried[3] + core_parts[2], carried[4] + core_parts[3],
                     carried[5].at[session].add(mask_grad),
                     carried[6].at[session].add(feat_grad),
                     carried[7].at[session].add(bias_grad))
        return new_carry, None

    start_carry = (jnp.zeros((), jnp.float32),
                   jnp.zeros((C, TAPS), jnp.float32), jnp.zeros((C,), jnp.float32),
                   jnp.zeros((C, C), jnp.float32), jnp.zeros((C,), jnp.float32),
                   jnp.zeros((SESSIONS, N, POOLED), jnp.float32),
                   jnp.zeros((SESSIONS, N, C), jnp.float32),
                   jnp.zeros((SESSIONS, N), jnp.float32))
    final, _ = lax.scan(one_clip, start_carry, (video, responses, assignment.astype(jnp.int32)))
    return (final[0], final[1], final[2], final[3], final[4], final[5], final[6], final[7])
```

```python
import functools

import jax
import jax.numpy as jnp
import numpy as np
from jax import lax
from jax.experimental import pallas as pl
from jax.experimental.pallas import tpu as pltpu
from jax.sharding import PartitionSpec as P

HH = 36
WW = 64
KS = 7
KT = 3
CH = 64
POOLED = 576
TAPS = 147
PLANES = 4
BASE_W = 768
ROWS = 16
NBLOCK = 512
GROWS = 648
F32 = jnp.float32
BF16 = jnp.bfloat16
VM = 56 * 2**20


def tap_tables():
    fold = np.zeros((4, 256, 256), np.float32)
    for a in range(2):
        for b in range(2):
            for dt in range(KT):
                for dy in range(KS):
                    for dx in range(KS):
                        u, v = dy + a, dx + b
                        depth = ((u // 2) * 4 + v // 2) * ROWS + dt * 4 + (u % 2) * 2 + v % 2
                        fold[a * 2 + b, depth, (dt * KS + dy) * KS + dx] = 1.0
            fold[a * 2 + b, 12, TAPS] = 1.0
    return fold


def split_table():
    table = np.zeros((512, 512), np.float32)
    for i in range(4):
        for ru in range(2):
            for x in range(WW):
                table[i * 128 + ru * 64 + x, (ru * 2 + x % 2) * 128 + i * 32 + x // 2] = 1.0
    return table


def dot(a, b, dims=((1,), (0,)), precision=None):
    return lax.dot_general(a, b, (dims, ((), ())), preferred_element_type=F32, precision=precision)


NT = ((1,), (1,))


def plane_offsets():
    return [66 - 32 * ru - rv for ru in (1, 0) for rv in (1, 0)]


def split_planes(video, table):
    blocks = [video[:, t * 512 : (t + 1) * 512] for t in range(4)]
    tail = jnp.concatenate([video[:, 2048:2304], jnp.zeros((16, 256), BF16)], axis=1)
    stacked = jnp.concatenate(blocks + [tail], axis=0)
    split = dot(stacked, table)
    out = []
    for plane, offset in enumerate(plane_offsets()):
        parts = [split[t * 16 : (t + 1) * 16, plane * 128 : (plane + 1) * 128] for t in range(5)]
        flat = jnp.concatenate(parts + [jnp.zeros((16, 128), F32)], axis=1)
        out.append(pltpu.roll(flat, offset, 1))
    return out[::-1]


def prep_kernel(video_ref, table_ref, planes_ref):
    planes = split_planes(video_ref[...], table_ref[...])
    planes_ref[...] = jnp.concatenate(planes, axis=0).astype(BF16)


def make_base(prev, own, after, tiled_assignment):
    stacked = jnp.concatenate([prev, own, after], axis=0)
    row = lax.broadcasted_iota(jnp.int32, (256, 192), 0)
    col = lax.broadcasted_iota(jnp.int32, (256, 192), 1)
    pick = (row % 16 == col // 16) & (tiled_assignment == row // 16)
    return dot(pick.astype(BF16), stacked)


def column_masks():
    row = lax.broadcasted_iota(jnp.int32, (ROWS, POOLED), 0)
    column = lax.broadcasted_iota(jnp.int32, (ROWS, POOLED), 1) % 32
    masks = []
    for shift in range(4):
        at = column + shift - 2 + row % 2
        masks.append((at >= 0) & (at < 32) & (row < 12))
    return masks


def fill_patches(base, patches_ref, masks):
    for qu in range(4):
        for qv in range(4):
            shift = qu * 32 + qv
            moved = base if shift == 0 else pltpu.roll(base, BASE_W - shift, 1)
            tile = jnp.where(masks[qv], moved[:, :POOLED], 0.0)
            if shift == 0:
                row = lax.broadcasted_iota(jnp.int32, (ROWS, POOLED), 0)
                tile = jnp.where(row == 12, 1.0, tile)
            at = (qu * 4 + qv) * ROWS
            patches_ref[at : at + ROWS, :] = tile.astype(BF16)


def conv_matrix(conv_weight, fold_ref, w2_ref):
    for ab in range(4):
        block = dot(conv_weight, fold_ref[ab].astype(BF16), NT)
        w2_ref[ab * CH : (ab + 1) * CH, :] = block.astype(BF16)


def activations(w2, patches, bias1, mix4, bias2):
    pre1 = dot(w2, patches) + bias1
    slope1 = jnp.exp(jnp.minimum(pre1, 0.0))
    act1 = jnp.where(pre1 > 0, pre1, slope1 - 1.0).astype(BF16)
    pre2 = dot(mix4, act1) + bias2
    slope2 = jnp.exp(jnp.minimum(pre2, 0.0))
    return slope1, act1, pre2, slope2


def forward_kernel(
    prev_ref, own_ref, after_ref, assign_ref, weight_ref, fold_ref, bias1_ref, mix_ref, bias2_ref,
    pooled_ref, base_ref, patches_ref, w2_ref,
):
    base_ref[...] = make_base(prev_ref[...], own_ref[...], after_ref[...], assign_ref[...])
    conv_matrix(weight_ref[...], fold_ref, w2_ref)
    masks = column_masks()

    def clip(k, carry):
        fill_patches(base_ref[pl.ds(pl.multiple_of(k * ROWS, ROWS), ROWS), :], patches_ref, masks)
        _, _, pre2, slope2 = activations(
            w2_ref[...], patches_ref[...], bias1_ref[...], mix_ref[...], bias2_ref[...]
        )
        feats = jnp.where(pre2 > 0, pre2, slope2 - 1.0).astype(BF16).astype(F32)
        total = feats[0:64] + feats[64:128] + feats[128:192] + feats[192:256]
        pooled_ref[k] = (total * 0.25).astype(BF16)
        return carry

    lax.fori_loop(0, 16, clip, 0)


def backward_kernel(
    prev_ref, own_ref, after_ref, assign_ref, weight_ref, fold_ref, bias1_ref, mix_ref, mix_t_ref, bias2_ref,
    grad_ref, loss_ref, small_ref, base_ref, patches_ref, w2_ref, gmix_ref, gconv_ref, gbias_ref,
):
    base_ref[...] = make_base(prev_ref[...], own_ref[...], after_ref[...], assign_ref[...])
    conv_matrix(weight_ref[...], fold_ref, w2_ref)
    masks = column_masks()
    gmix_ref[...] = jnp.zeros_like(gmix_ref)
    gconv_ref[...] = jnp.zeros_like(gconv_ref)
    gbias_ref[...] = jnp.zeros_like(gbias_ref)

    def clip(k, carry):
        fill_patches(base_ref[pl.ds(pl.multiple_of(k * ROWS, ROWS), ROWS), :], patches_ref, masks)
        patches = patches_ref[...]
        slope1, act1, _, slope2 = activations(
            w2_ref[...], patches, bias1_ref[...], mix_ref[...], bias2_ref[...]
        )
        grad = grad_ref[k].astype(F32) * 0.25
        grad4 = jnp.concatenate([grad] * 4, axis=0)
        pre2_grad = (grad4 * slope2).astype(BF16)
        gmix_ref[...] += dot(pre2_grad, act1, NT)
        gbias_ref[...] += jnp.sum(pre2_grad.astype(F32), axis=1, keepdims=True)
        pre1_grad = (dot(mix_t_ref[...], pre2_grad) * slope1).astype(BF16)
        gconv_ref[...] += dot(pre1_grad, patches, NT)
        return carry

    lax.fori_loop(0, 16, clip, 0)
    finish_small(gmix_ref, gconv_ref, gbias_ref, fold_ref, loss_ref[...], small_ref)


def finish_small(gmix_ref, gconv_ref, gbias_ref, fold_ref, loss, small_ref):
    row = lax.broadcasted_iota(jnp.int32, (256, 256), 0)
    col = lax.broadcasted_iota(jnp.int32, (256, 256), 1)
    total = jnp.zeros((CH, 256), F32)
    bias = jnp.zeros((CH, 1), F32)
    for ab in range(4):
        rows = slice(ab * CH, (ab + 1) * CH)
        place = ((row // CH == ab) & (col == row % CH + TAPS + 1)).astype(F32)
        total += dot(gconv_ref[rows, :], fold_ref[ab], precision=lax.Precision.HIGHEST)
        total += dot(gmix_ref[rows, :], place, precision=lax.Precision.HIGHEST)
        bias += gbias_ref[rows, :]
    lane = lax.broadcasted_iota(jnp.int32, (CH, 256), 1)
    line = lax.broadcasted_iota(jnp.int32, (CH, 256), 0)
    total = jnp.where(lane == TAPS + 1 + CH, bias, total)
    total = jnp.where((lane == TAPS + 2 + CH) & (line == 0), loss, total)
    small_ref[...] = total


def readout_kernel(
    loss_scale, count_ref, pooled_ref, mask_ref, weight_ref, rbias_ref, target_ref,
    grads_ref, back_ref, loss_ref, turned_ref, proj_ref, mixed_ref, total_ref,
):
    step = pl.program_id(0)

    @pl.when(step == 0)
    def _():
        turned_ref[...] = pooled_ref[...].T
        total_ref[...] = jnp.zeros_like(total_ref)
        loss_ref[...] = jnp.zeros_like(loss_ref)

    mask = mask_ref[...]
    weight = weight_ref[...].astype(F32).T
    proj_ref[...] = dot(pooled_ref[...], mask, NT)
    drives = []
    for f in range(16):
        drives.append(jnp.sum(proj_ref[f * CH : (f + 1) * CH, :] * weight, axis=0, keepdims=True))
    drive = jnp.concatenate(drives, axis=0) + rbias_ref[...]
    target = target_ref[...].astype(F32)
    small = jnp.exp(-jnp.abs(drive))
    rate = jnp.maximum(drive, 0.0) + jnp.log1p(small) + 0.1
    sigmoid = jnp.where(drive >= 0, 1.0, small) / (1.0 + small)
    slot = step * NBLOCK + lax.broadcasted_iota(jnp.int32, (16, NBLOCK), 1)
    alive = slot < count_ref[0]
    loss_ref[...] += jnp.sum(jnp.where(alive, rate - target * jnp.log(rate), 0.0), keepdims=True) * loss_scale
    grad_drive = jnp.where(alive, (1.0 - target / rate) * sigmoid, 0.0) * loss_scale
    feat = jnp.zeros((CH, NBLOCK), F32)
    for f in range(16):
        line = grad_drive[f : f + 1, :]
        feat += line * proj_ref[f * CH : (f + 1) * CH, :]
        mixed_ref[f * CH : (f + 1) * CH, :] = (line * weight).astype(BF16)
    grads_ref[0, POOLED : POOLED + CH, :] = feat
    bias_grad = jnp.sum(grad_drive, axis=0, keepdims=True)
    grads_ref[0, POOLED + CH : GROWS, :] = jnp.broadcast_to(bias_grad, (GROWS - POOLED - CH, NBLOCK))
    mixed = mixed_ref[...]
    grads_ref[0, 0:POOLED, :] = dot(turned_ref[...], mixed)
    total_ref[...] += dot(mixed, mask)

    @pl.when(step == pl.num_programs(0) - 1)
    def _():
        back_ref[...] = total_ref[...].astype(BF16)


def params():
    return pltpu.CompilerParams(vmem_limit_bytes=VM)


def run_prep(video, table):
    return pl.pallas_call(
        prep_kernel,
        out_shape=jax.ShapeDtypeStruct((64, BASE_W), BF16),
        compiler_params=params(),
        name="prep",
    )(video, table)


def run_forward(*args):
    return pl.pallas_call(
        forward_kernel,
        out_shape=jax.ShapeDtypeStruct((16, CH, POOLED), BF16),
        scratch_shapes=[
            pltpu.VMEM((256, BASE_W), F32),
            pltpu.VMEM((256, POOLED), BF16),
            pltpu.VMEM((256, 256), BF16),
        ],
        compiler_params=params(),
        name="core_forward",
    )(*args)


def run_backward(*args):
    return pl.pallas_call(
        backward_kernel,
        out_shape=jax.ShapeDtypeStruct((CH, 256), F32),
        scratch_shapes=[
            pltpu.VMEM((256, BASE_W), F32),
            pltpu.VMEM((256, POOLED), BF16),
            pltpu.VMEM((256, 256), BF16),
            pltpu.VMEM((256, 256), F32),
            pltpu.VMEM((256, 256), F32),
            pltpu.VMEM((256, 1), F32),
        ],
        compiler_params=params(),
        name="core_backward",
    )(*args)


def run_readout(loss_scale, count, pooled, masks, weight, rbias, target):
    neurons = masks.shape[0]
    steps = neurons // NBLOCK
    return pl.pallas_call(
        functools.partial(readout_kernel, loss_scale),
        grid=(steps,),
        in_specs=[
            pl.BlockSpec(memory_space=pltpu.SMEM),
            pl.BlockSpec((1024, POOLED), lambda i: (0, 0)),
            pl.BlockSpec((NBLOCK, POOLED), lambda i: (i, 0)),
            pl.BlockSpec((NBLOCK, CH), lambda i: (i, 0)),
            pl.BlockSpec((1, NBLOCK), lambda i: (0, i)),
            pl.BlockSpec((16, NBLOCK), lambda i: (0, i)),
        ],
        out_specs=[
            pl.BlockSpec((1, GROWS, NBLOCK), lambda i: (i, 0, 0)),
            pl.BlockSpec((1024, POOLED), lambda i: (0, 0)),
            pl.BlockSpec((1, 1), lambda i: (0, 0)),
        ],
        out_shape=[
            jax.ShapeDtypeStruct((steps, GROWS, NBLOCK), F32),
            jax.ShapeDtypeStruct((1024, POOLED), BF16),
            jax.ShapeDtypeStruct((1, 1), F32),
        ],
        scratch_shapes=[
            pltpu.VMEM((POOLED, 1024), BF16),
            pltpu.VMEM((1024, NBLOCK), F32),
            pltpu.VMEM((1024, NBLOCK), BF16),
            pltpu.VMEM((1024, POOLED), F32),
        ],
        compiler_params=params(),
        name="readout",
    )(count, pooled, masks, weight, rbias, target)


def per_device(
    video, responses, assignment, counts, conv_weight, conv_bias, mix_weight, mix_bias, masks, feat_w, readout_bias,
):
    sess_total = lax.axis_size("sess")
    clip_total = lax.axis_size("clip")
    loss_scale = 1.0 / (video.shape[0] * clip_total * sess_total)
    own = run_prep(video[:, 0, :], jnp.asarray(split_table(), BF16))
    up = [(i, i + 1) for i in range(sess_total - 1)]
    down = [(j, i) for i, j in up]
    prev = lax.ppermute(own, "sess", up)
    after = lax.ppermute(own, "sess", down)
    tiled_assignment = jnp.tile(assignment, 12)[None]
    pick = (assignment[None, :] == jnp.arange(16, dtype=jnp.int32)[:, None]).astype(BF16)
    target = jnp.dot(pick, responses[:, 0, :], preferred_element_type=F32).astype(BF16)
    target = lax.all_to_all(target, "sess", split_axis=0, concat_axis=0, tiled=True)
    weight = jnp.pad(conv_weight, ((0, 0), (0, 256 - TAPS)))
    fold = jnp.asarray(tap_tables())
    eye = jnp.eye(4, dtype=BF16)
    mix4 = jnp.kron(eye, mix_weight)
    mix4_t = jnp.kron(eye, mix_weight.T)
    bias1 = jnp.tile(conv_bias, 4)[:, None]
    bias2 = jnp.tile(mix_bias, 4)[:, None]
    core = (prev, own, after, tiled_assignment, weight, fold, bias1)
    pooled = run_forward(*core, mix4, bias2)
    received = lax.all_to_all(pooled, "sess", split_axis=0, concat_axis=0, tiled=True)
    grads, back, loss = run_readout(
        loss_scale, counts, received.reshape(1024, POOLED), masks[0], feat_w[0], readout_bias, target
    )
    summed = lax.psum_scatter(grads, "clip", scatter_dimension=0, tiled=True)
    returned = lax.all_to_all(back.reshape(16, CH, POOLED), "sess", split_axis=0, concat_axis=0, tiled=True)
    small = run_backward(*core, mix4, mix4_t, bias2, returned, loss)
    small = lax.psum(small, ("clip", "sess"))
    turned = summed[0].T
    return (
        small[0, TAPS + 2 + CH],
        small[:, :TAPS],
        small[:, TAPS],
        small[:, TAPS + 1 : TAPS + 1 + CH],
        small[:, TAPS + 1 + CH],
        turned[None, :, :POOLED],
        turned[None, :, POOLED : POOLED + CH],
        turned[None, :, POOLED + CH],
    )


def solution(mesh):
    return jax.shard_map(
        per_device,
        mesh=mesh,
        in_specs=(
            P("clip", "sess", None),
            P("clip", "sess", None),
            P("clip"),
            P("sess"),
            P(),
            P(),
            P(),
            P(),
            P("sess", None, None),
            P("sess", None, None),
            P("sess", None),
        ),
        out_specs=(
            P(),
            P(),
            P(),
            P(),
            P(),
            P("sess", "clip", None),
            P("sess", "clip", None),
            P("sess", "clip"),
        ),
        check_vma=False,
    )
```

```python
import functools

import jax
import jax.numpy as jnp
import numpy as np
from jax import lax
from jax.experimental import pallas as pl
from jax.experimental.pallas import tpu as pltpu
from jax.sharding import PartitionSpec as P

HH = 36
WW = 64
KS = 7
KT = 3
CH = 64
POOLED = 576
TAPS = 147
BASE_W = 768
ROWS = 16
NBLOCK = 512
GROWS = 648
F32 = jnp.float32
BF16 = jnp.bfloat16
VM = 60 * 2**20
LOW = 328
MESH = pl.DeviceIdType.MESH


def tap_tables():
    fold = np.zeros((4, 256, 256), np.float32)
    for a in range(2):
        for b in range(2):
            for dt in range(KT):
                for dy in range(KS):
                    for dx in range(KS):
                        u, v = dy + a, dx + b
                        depth = ((u // 2) * 4 + v // 2) * ROWS + dt * 4 + (u % 2) * 2 + v % 2
                        fold[a * 2 + b, depth, (dt * KS + dy) * KS + dx] = 1.0
            fold[a * 2 + b, 12, TAPS] = 1.0
    return fold


def split_table():
    table = np.zeros((512, 512), np.float32)
    for i in range(4):
        for ru in range(2):
            for x in range(WW):
                table[i * 128 + ru * 64 + x, (ru * 2 + x % 2) * 128 + i * 32 + x // 2] = 1.0
    return table


def dot(a, b, dims=((1,), (0,)), precision=None):
    return lax.dot_general(a, b, (dims, ((), ())), preferred_element_type=F32, precision=precision)


NT = ((1,), (1,))


def plane_offsets():
    return [66 - 32 * ru - rv for ru in (1, 0) for rv in (1, 0)]


def split_planes(video, table):
    blocks = [video[:, t * 512 : (t + 1) * 512] for t in range(4)]
    tail = jnp.concatenate([video[:, 2048:2304], jnp.zeros((16, 256), BF16)], axis=1)
    stacked = jnp.concatenate(blocks + [tail], axis=0)
    split = dot(stacked, table)
    out = []
    for plane, offset in enumerate(plane_offsets()):
        parts = [split[t * 16 : (t + 1) * 16, plane * 128 : (plane + 1) * 128] for t in range(5)]
        flat = jnp.concatenate(parts + [jnp.zeros((16, 128), F32)], axis=1)
        out.append(pltpu.roll(flat, offset, 1))
    return out[::-1]


def column_masks():
    row = lax.broadcasted_iota(jnp.int32, (ROWS, POOLED), 0)
    column = lax.broadcasted_iota(jnp.int32, (ROWS, POOLED), 1) % 32
    masks = []
    for shift in range(4):
        at = column + shift - 2 + row % 2
        masks.append((at >= 0) & (at < 32) & (row < 12))
    return masks


def fill_patches(base, patches_ref, k, masks):
    for qu in range(4):
        for qv in range(4):
            shift = qu * 32 + qv
            moved = base if shift == 0 else pltpu.roll(base, BASE_W - shift, 1)
            tile = jnp.where(masks[qv], moved[:, :POOLED], 0.0)
            if shift == 0:
                row = lax.broadcasted_iota(jnp.int32, (ROWS, POOLED), 0)
                tile = jnp.where(row == 12, 1.0, tile)
            at = (qu * 4 + qv) * ROWS
            patches_ref[k, at : at + ROWS, :] = tile.astype(BF16)


def conv_matrix(conv_weight, fold_ref, w2_ref):
    for ab in range(4):
        block = dot(conv_weight, fold_ref[ab][:, :TAPS], NT)
        w2_ref[ab * CH : (ab + 1) * CH, :] = block.astype(BF16)


def remote(src, dst, sends, recvs, send_at, recv_at, peer):
    return pltpu.make_async_remote_copy(
        src_ref=src, dst_ref=dst, send_sem=sends.at[send_at], recv_sem=recvs.at[recv_at],
        device_id=peer, device_id_type=MESH,
    )


def iotas(shape):
    return lax.broadcasted_iota(jnp.int32, shape, 0), lax.broadcasted_iota(jnp.int32, shape, 1)


def one_hot(condition):
    return jnp.where(condition, 1.0, 0.0)


def sorting_matrix(assignment):
    row, _ = iotas((16, 16))
    pick = one_hot(assignment == row)
    row, col = iotas((16, 256))
    wide = dot(pick, one_hot(col % 16 == row))
    row, col = iotas((256, 16))
    tall = dot(one_hot(row // 16 == col), wide)
    row, col = iotas((256, 256))
    return jnp.where(row % 16 == col // 16, tall, 0.0).astype(BF16)


def column(line):
    row, col = iotas((CH, CH))
    one = jnp.sum(jnp.where(row == col, line, 0.0), axis=1, keepdims=True)
    return jnp.concatenate([one] * 4, axis=0)


def block_diagonal(matrix):
    row, col = iotas((CH, 256))
    wide = dot(matrix.astype(BF16), one_hot(col % CH == row).astype(BF16))
    row, col = iotas((256, 256))
    return jnp.where(row // CH == col // CH, jnp.concatenate([wide] * 4, axis=0), 0.0).astype(BF16)


def elu(values):
    return jnp.where(values > 0, values, jnp.exp(jnp.minimum(values, 0.0)) - 1.0)


def finish_small(gmix_ref, gconv_ref, gbias_ref, fold_ref, loss):
    row, col = iotas((256, 256))
    total = jnp.zeros((CH, 256), F32)
    bias = jnp.zeros((CH, 1), F32)
    for ab in range(4):
        rows = slice(ab * CH, (ab + 1) * CH)
        place = one_hot((row // CH == ab) & (col == row % CH + TAPS + 1))
        total += dot(gconv_ref[rows, :], fold_ref[ab].astype(F32), precision=lax.Precision.HIGHEST)
        total += dot(gmix_ref[rows, :], place, precision=lax.Precision.HIGHEST)
        bias += gbias_ref[rows, :]
    line, lane = iotas((CH, 256))
    total = jnp.where(lane == TAPS + 1 + CH, bias, total)
    return jnp.where((lane == TAPS + 2 + CH) & (line == 0), loss, total)


def step_kernel(
    loss_scale,
    count_ref, video_ref, responses_ref, assign_ref, weight_ref, bias1_ref, mix_ref, bias2_ref,
    masks_hbm, featw_hbm, rbias_ref, table_ref, fold_ref,
    loss_out, conv_out, convb_out, mix_out, mixb_out, gmask_out, gfeat_out, gbias_out,
    mask_ref, featw_ref, planes_ref, prev_ref, after_ref, base_ref, w2_ref, mix4_ref, mixt_ref,
    patches_ref, act_ref, feats_ref, psend_ref, precv_ref, tsend_ref, trecv_ref, target_ref,
    turned_ref, proj_ref, mixed_ref, total_ref, loss_ref,
    blocks_ref, got_ref, low_ref, up_ref, minus_ref, plus_ref, bsend_ref, brecv_ref,
    gmix_ref, gconv_ref, gmixb_ref, ar_ref, r1_ref, s2_ref, r2_ref, s3_ref, r3_ref,
    local_sem, halo_s, halo_r, pool_s, pool_r, targ_s, targ_r, pair_s, pair_r, ring_s, ring_r,
    back_s, back_r, a1_s, a1_r, a2_s, a2_r, a3_s, a3_r,
):
    sess = lax.axis_index("sess")
    clip = lax.axis_index("clip")
    row_y = clip // 2
    core = clip % 2

    mask_copy = pltpu.make_async_copy(masks_hbm.at[0], mask_ref, local_sem.at[0])
    featw_copy = pltpu.make_async_copy(featw_hbm.at[0], featw_ref, local_sem.at[1])
    mask_copy.start()
    featw_copy.start()

    barrier = pltpu.get_barrier_semaphore()

    def greet_sess(j, carry):
        pl.semaphore_signal(barrier, inc=1, device_id={"sess": (sess + j) % 16}, device_id_type=MESH)
        return carry

    def greet_clip(j, carry):
        pl.semaphore_signal(barrier, inc=1, device_id={"clip": (clip + j) % 8}, device_id_type=MESH)
        return carry

    lax.fori_loop(1, 16, greet_sess, 0)
    lax.fori_loop(1, 8, greet_clip, 0)

    planes = split_planes(video_ref[...], table_ref[...])
    planes_ref[...] = jnp.concatenate(planes, axis=0).astype(BF16)
    pl.semaphore_wait(barrier, 22)

    halo_up = remote(planes_ref, prev_ref, halo_s, halo_r, 0, 0, {"sess": (sess + 1) % 16})
    halo_down = remote(planes_ref, after_ref, halo_s, halo_r, 1, 1, {"sess": (sess + 15) % 16})
    halo_up.start()
    halo_down.start()

    sort = sorting_matrix(assign_ref[...])
    stacked = jnp.concatenate([responses_ref[:, q * 256 : (q + 1) * 256] for q in range(16)], axis=0)
    tsend_ref[...] = dot(sort, stacked).astype(BF16).reshape(16, 16, 256)

    def target_copy(j):
        peer = (sess + 1 + j) % 16
        return remote(tsend_ref.at[peer], trecv_ref.at[sess], targ_s, targ_r, peer, sess, {"sess": peer})

    def start_target(j, carry):
        target_copy(j).start()
        return carry

    lax.fori_loop(0, 15, start_target, 0)
    trecv_ref[sess] = tsend_ref[sess]

    conv_matrix(weight_ref[...], fold_ref, w2_ref)
    mix = mix_ref[...].astype(F32)
    mix4_ref[...] = block_diagonal(mix)
    mixt_ref[...] = block_diagonal(mix.T)
    bias1 = column(bias1_ref[...])
    bias2 = column(bias2_ref[...])
    masks = column_masks()

    halo_up.wait()
    halo_down.wait()
    none = jnp.zeros((64, BASE_W), BF16)
    prev = jnp.where(sess == 0, none, prev_ref[...])
    after = jnp.where(sess == 15, none, after_ref[...])
    window = jnp.concatenate([prev, planes_ref[...], after], axis=0)
    base_ref[...] = dot(sort[:, :192], window)

    def pooled_copy(j):
        peer = (sess + 1 + j) % 16
        return remote(psend_ref.at[peer], precv_ref.at[sess], pool_s, pool_r, peer, sess, {"sess": peer})

    def forward(j, carry):
        k = (sess + 1 + j) % 16
        fill_patches(base_ref[pl.ds(pl.multiple_of(k * ROWS, ROWS), ROWS), :], patches_ref, k, masks)
        act1 = elu(dot(w2_ref[...], patches_ref[k]) + bias1).astype(BF16)
        act_ref[k] = act1
        feats = elu(dot(mix4_ref[...], act1) + bias2).astype(BF16)
        feats_ref[k] = feats
        wide = feats.astype(F32)
        total = wide[0:64] + wide[64:128] + wide[128:192] + wide[192:256]
        psend_ref[k] = (total * 0.25).astype(BF16)

        @pl.when(j < 15)
        def _():
            pooled_copy(j).start()

        return carry

    lax.fori_loop(0, 16, forward, 0)
    precv_ref[sess] = psend_ref[sess]
    total_ref[...] = jnp.zeros_like(total_ref)
    loss_ref[...] = jnp.zeros_like(loss_ref)
    gmix_ref[...] = jnp.zeros_like(gmix_ref)
    gconv_ref[...] = jnp.zeros_like(gconv_ref)
    gmixb_ref[...] = jnp.zeros_like(gmixb_ref)
    mask_copy.wait()
    featw_copy.wait()

    def wait_forward(j, carry):
        peer = (sess + 15 - j) % 16
        there = (sess + 1 + j) % 16
        remote(psend_ref.at[there], precv_ref.at[peer], pool_s, pool_r, there, peer, {"sess": there}).wait()
        remote(tsend_ref.at[there], trecv_ref.at[peer], targ_s, targ_r, there, peer, {"sess": there}).wait()
        return carry

    lax.fori_loop(0, 15, wait_forward, 0)

    row, col = iotas((256, 256))
    swap = one_hot((row // 16 == col % 16) & (row % 16 == col // 16)).astype(BF16)
    target_ref[...] = dot(swap, trecv_ref[...].reshape(256, 256))
    turned_ref[...] = precv_ref[...].reshape(1024, POOLED).T

    partner = {"clip": row_y * 2 + 1 - core}
    right = {"clip": (row_y + 1) % 4 * 2 + core}
    left = {"clip": (row_y + 3) % 4 * 2 + core}
    high = GROWS - LOW

    def pair_copy(t):
        return remote(blocks_ref.at[t], got_ref.at[t], pair_s, pair_r, t, t, partner)

    def ring_copy(src, dst, at, peer):
        return remote(src, dst, ring_s, ring_r, at, at, peer)

    def lows(ref):
        return ref.at[pl.ds(0, LOW)]

    def highs(ref):
        return ref.at[pl.ds(LOW, high)]

    two = blocks_ref.at[4 + (row_y + 2) % 4]
    one = blocks_ref.at[4 + (row_y + 1) % 4]
    three = blocks_ref.at[4 + (row_y + 3) % 4]
    relay_low = ring_copy(lows(two), low_ref, 0, right)
    relay_high = ring_copy(highs(two), up_ref, 1, left)
    right_high = ring_copy(highs(one), highs(minus_ref), 2, right)
    left_low = ring_copy(lows(three), lows(plus_ref), 3, left)
    right_low = ring_copy(lows(one), lows(minus_ref), 4, right)
    left_high = ring_copy(highs(three), highs(plus_ref), 5, left)

    def readout(slot, n):
        mask = mask_ref[pl.ds(pl.multiple_of(n * NBLOCK, NBLOCK), NBLOCK), :]
        weight = featw_ref[pl.ds(pl.multiple_of(n * NBLOCK, NBLOCK), NBLOCK), :].astype(F32).T
        proj_ref[...] = dot(precv_ref[...].reshape(1024, POOLED), mask, NT)
        drives = []
        for f in range(16):
            drives.append(jnp.sum(proj_ref[f * CH : (f + 1) * CH, :] * weight, axis=0, keepdims=True))
        at = pl.ds(pl.multiple_of(n * NBLOCK, NBLOCK), NBLOCK)
        drive = jnp.concatenate(drives, axis=0) + rbias_ref[:, at]
        first = target_ref[pl.ds(pl.multiple_of(n * 32, 32), 16), :]
        second = target_ref[pl.ds(pl.multiple_of(n * 32 + 16, 16), 16), :]
        target = jnp.concatenate([first, second], axis=1)
        small = jnp.exp(-jnp.abs(drive))
        rate = jnp.maximum(drive, 0.0) + jnp.log1p(small) + 0.1
        sigmoid = jnp.where(drive >= 0, 1.0, small) / (1.0 + small)
        place = n * NBLOCK + lax.broadcasted_iota(jnp.int32, (16, NBLOCK), 1)
        alive = place < count_ref[0]
        terms = jnp.where(alive, rate - target * jnp.log(rate), 0.0)
        loss_ref[...] += jnp.sum(terms, keepdims=True) * loss_scale
        grad_drive = jnp.where(alive, (1.0 - target / rate) * sigmoid, 0.0) * loss_scale
        feat = jnp.zeros((CH, NBLOCK), F32)
        for f in range(16):
            line = grad_drive[f : f + 1, :]
            feat += line * proj_ref[f * CH : (f + 1) * CH, :]
            mixed_ref[f * CH : (f + 1) * CH, :] = (line * weight).astype(BF16)
        blocks_ref[slot, POOLED : POOLED + CH, :] = feat
        bias_grad = jnp.sum(grad_drive, axis=0, keepdims=True)
        blocks_ref[slot, POOLED + CH : GROWS, :] = jnp.broadcast_to(bias_grad, (GROWS - POOLED - CH, NBLOCK))
        mixed = mixed_ref[...]
        blocks_ref[slot, 0:POOLED, :] = dot(turned_ref[...], mixed)
        total_ref[...] += dot(mixed, mask)

    def phase(i, carry):
        t = (row_y + jnp.where(i == 0, 2, jnp.where(i == 1, 1, jnp.where(i == 2, 3, 0)))) % 4

        def half(h, inner):
            readout(h * 4 + t, t * 2 + jnp.where(h == 0, 1 - core, core))

            @pl.when(h == 0)
            def _():
                pair_copy(t).start()

            return inner

        lax.fori_loop(0, 2, half, 0)
        pair_copy(t).wait()
        blocks_ref[4 + t] += got_ref[t]

        @pl.when(i == 0)
        def _():
            relay_low.start()
            relay_high.start()

        @pl.when(i == 1)
        def _():
            right_high.start()

        @pl.when(i == 2)
        def _():
            left_low.start()

        return carry

    lax.fori_loop(0, 4, phase, 0)

    def back_copy(j):
        peer = (sess + 1 + j) % 16
        return remote(bsend_ref.at[peer], brecv_ref.at[sess], back_s, back_r, peer, sess, {"sess": peer})

    def send_back(j, carry):
        f = (sess + 1 + j) % 16
        bsend_ref[f] = total_ref[pl.ds(pl.multiple_of(f * CH, CH), CH), :].astype(BF16)

        @pl.when(j < 15)
        def _():
            back_copy(j).start()

        return carry

    lax.fori_loop(0, 16, send_back, 0)
    brecv_ref[sess] = bsend_ref[sess]

    relay_low.wait()
    blocks_ref[4 + (row_y + 1) % 4, 0:LOW, :] += low_ref[...]
    right_low.start()
    relay_high.wait()
    blocks_ref[4 + (row_y + 3) % 4, LOW:GROWS, :] += up_ref[...]
    left_high.start()

    def backward(j, carry):
        k = (sess + 15 - j) % 16
        there = (sess + 1 + j) % 16

        @pl.when(j < 15)
        def _():
            remote(bsend_ref.at[there], brecv_ref.at[k], back_s, back_r, there, k, {"sess": there}).wait()

        grad = brecv_ref[k].astype(F32) * 0.25
        slope2 = 1.0 + jnp.minimum(feats_ref[k].astype(F32), 0.0)
        pre2_grad = (jnp.concatenate([grad] * 4, axis=0) * slope2).astype(BF16)
        act1 = act_ref[k]
        gmix_ref[...] += dot(pre2_grad, act1, NT)
        gmixb_ref[...] += jnp.sum(pre2_grad.astype(F32), axis=1, keepdims=True)
        slope1 = 1.0 + jnp.minimum(act1.astype(F32), 0.0)
        pre1_grad = (dot(mixt_ref[...], pre2_grad) * slope1).astype(BF16)
        gconv_ref[...] += dot(pre1_grad, patches_ref[k], NT)
        return carry

    lax.fori_loop(0, 16, backward, 0)

    small = finish_small(gmix_ref, gconv_ref, gmixb_ref, fold_ref, loss_ref[...])
    for piece in range(16):
        top, lane = piece // 2 * 8, piece % 2 * 128
        ar_ref[piece] = small[top : top + 8, lane : lane + 128]

    def a1_copy(j, here):
        peer = (sess + 1 + j) % 16
        return remote(ar_ref.at[peer], r1_ref.at[here], a1_s, a1_r, peer, here, {"sess": peer})

    def a2_copy(j, here):
        peer = (clip + 1 + j) % 8
        return remote(s2_ref, r2_ref.at[here], a2_s, a2_r, peer, here, {"clip": peer})

    def a3_copy(j, here):
        peer = (sess + 1 + j) % 16
        return remote(s3_ref, r3_ref.at[here], a3_s, a3_r, peer, here, {"sess": peer})

    def exchange(copy, count, mine):
        def begin(j, carry):
            copy(j, mine).start()
            return carry

        def finish(j, carry):
            copy(j, (mine + count - j) % (count + 1)).wait()
            return carry

        lax.fori_loop(0, count, begin, 0)
        lax.fori_loop(0, count, finish, 0)

    r1_ref[sess] = ar_ref[sess]
    exchange(a1_copy, 15, sess)
    part = jnp.sum(r1_ref[...], axis=0)
    s2_ref[...] = part
    r2_ref[clip] = part
    exchange(a2_copy, 7, clip)
    part = jnp.sum(r2_ref[...], axis=0)
    s3_ref[...] = part
    r3_ref[sess] = part
    exchange(a3_copy, 15, sess)
    lines = [jnp.concatenate([r3_ref[2 * r], r3_ref[2 * r + 1]], axis=1) for r in range(8)]
    small = jnp.concatenate(lines, axis=0)
    conv_out[...] = small[:, :TAPS]
    row, col = iotas((CH, CH))
    convb_out[...] = jnp.sum(jnp.where(row == col, small[:, TAPS : TAPS + 1], 0.0), axis=0, keepdims=True)
    mix_out[...] = small[:, TAPS + 1 : TAPS + 1 + CH]
    mixb = small[:, TAPS + 1 + CH : TAPS + 2 + CH]
    mixb_out[...] = jnp.sum(jnp.where(row == col, mixb, 0.0), axis=0, keepdims=True)
    loss_out[...] = small[0:1, TAPS + 2 + CH : TAPS + 3 + CH]

    right_high.wait()
    left_low.wait()
    right_low.wait()
    left_high.wait()
    mine = blocks_ref[4 + row_y] + minus_ref[...] + plus_ref[...]
    gmask_out[...] = mine[0:POOLED].T
    gfeat_out[...] = mine[POOLED : POOLED + CH].T
    gbias_out[...] = mine[POOLED + CH : POOLED + CH + 1]


def run_step(loss_scale, *args):
    def vmem(shape, dtype):
        return pltpu.VMEM(shape, dtype)

    def dma(n):
        return pltpu.SemaphoreType.DMA((n,))

    whole = pl.BlockSpec(memory_space=pltpu.VMEM)
    anywhere = pl.BlockSpec(memory_space=pl.ANY)
    smem = pl.BlockSpec(memory_space=pltpu.SMEM)
    outs = [(1, 1), (CH, TAPS), (1, CH), (CH, CH), (1, CH), (NBLOCK, POOLED), (NBLOCK, CH), (1, NBLOCK)]
    neurons = args[8].shape[1]
    return pl.pallas_call(
        functools.partial(step_kernel, loss_scale),
        in_specs=[smem] + [whole] * 7 + [anywhere] * 2 + [whole] * 3,
        out_specs=[whole] * 8,
        out_shape=[jax.ShapeDtypeStruct(shape, F32) for shape in outs],
        scratch_shapes=[
            vmem((neurons, POOLED), BF16),
            vmem((neurons, CH), BF16),
            vmem((64, BASE_W), BF16),
            vmem((64, BASE_W), BF16),
            vmem((64, BASE_W), BF16),
            vmem((256, BASE_W), F32),
            vmem((256, 256), BF16),
            vmem((256, 256), BF16),
            vmem((256, 256), BF16),
            vmem((16, 256, POOLED), BF16),
            vmem((16, 256, POOLED), BF16),
            vmem((16, 256, POOLED), BF16),
            vmem((16, CH, POOLED), BF16),
            vmem((16, CH, POOLED), BF16),
            vmem((16, 16, 256), BF16),
            vmem((16, 16, 256), BF16),
            vmem((256, 256), F32),
            vmem((POOLED, 1024), BF16),
            vmem((1024, NBLOCK), F32),
            vmem((1024, NBLOCK), BF16),
            vmem((1024, POOLED), F32),
            vmem((1, 1), F32),
            vmem((8, GROWS, NBLOCK), F32),
            vmem((4, GROWS, NBLOCK), F32),
            vmem((LOW, NBLOCK), F32),
            vmem((GROWS - LOW, NBLOCK), F32),
            vmem((GROWS, NBLOCK), F32),
            vmem((GROWS, NBLOCK), F32),
            vmem((16, CH, POOLED), BF16),
            vmem((16, CH, POOLED), BF16),
            vmem((256, 256), F32),
            vmem((256, 256), F32),
            vmem((256, 1), F32),
            vmem((16, 8, 128), F32),
            vmem((16, 8, 128), F32),
            vmem((8, 128), F32),
            vmem((8, 8, 128), F32),
            vmem((8, 128), F32),
            vmem((16, 8, 128), F32),
        ]
        + [dma(n) for n in (2, 2, 2, 16, 16, 16, 16, 4, 4, 6, 6, 16, 16, 16, 16, 8, 8, 16, 16)],
        compiler_params=pltpu.CompilerParams(
            collective_id=0, has_side_effects=True, vmem_limit_bytes=VM
        ),
        name="train_step",
    )(*args)


def per_device(
    video, responses, assignment, counts, conv_weight, conv_bias, mix_weight, mix_bias, masks, feat_w, readout_bias,
):
    sess_total = lax.axis_size("sess")
    clip_total = lax.axis_size("clip")
    loss_scale = 1.0 / (video.shape[0] * clip_total * sess_total)
    loss, gconv, gconvb, gmix, gmixb, gmask, gfeat, gbias = run_step(
        loss_scale,
        counts,
        video.reshape(video.shape[0], -1),
        responses.reshape(responses.shape[0], -1),
        assignment[None],
        conv_weight,
        conv_bias[None],
        mix_weight,
        mix_bias[None],
        masks,
        feat_w,
        readout_bias,
        jnp.asarray(split_table(), BF16),
        jnp.asarray(tap_tables(), BF16),
    )
    return (
        loss[0, 0],
        gconv,
        gconvb[0],
        gmix,
        gmixb[0],
        gmask[None],
        gfeat[None],
        gbias,
    )


def solution(mesh):
    return jax.shard_map(
        per_device,
        mesh=mesh,
        in_specs=(
            P("clip", "sess", None),
            P("clip", "sess", None),
            P("clip"),
            P("sess"),
            P(),
            P(),
            P(),
            P(),
            P("sess", None, None),
            P("sess", None, None),
            P("sess", None),
        ),
        out_specs=(
            P(),
            P(),
            P(),
            P(),
            P(),
            P("sess", "clip", None),
            P("sess", "clip", None),
            P("sess", "clip"),
        ),
        check_vma=False,
    )
```

```python
import functools

import jax
import jax.numpy as jnp
import numpy as np
from jax import lax
from jax.experimental import pallas as pl
from jax.experimental.pallas import tpu as pltpu
from jax.sharding import PartitionSpec as P

HH = 36
WW = 64
KS = 7
KT = 3
CH = 64
POOLED = 576
TAPS = 147
BASE_W = 768
ROWS = 16
NBLOCK = 512
GROWS = 656
F32 = jnp.float32
BF16 = jnp.bfloat16
VM = 60 * 2**20
LOW = 336
GROUP = 2
MESH = pl.DeviceIdType.MESH


def tap_tables():
    fold = np.zeros((4, 256, 256), np.float32)
    for a in range(2):
        for b in range(2):
            for dt in range(KT):
                for dy in range(KS):
                    for dx in range(KS):
                        u, v = dy + a, dx + b
                        depth = ((u // 2) * 4 + v // 2) * ROWS + dt * 4 + (u % 2) * 2 + v % 2
                        fold[a * 2 + b, depth, (dt * KS + dy) * KS + dx] = 1.0
            fold[a * 2 + b, 12, TAPS] = 1.0
    return fold


def split_table():
    table = np.zeros((512, 512), np.float32)
    for i in range(4):
        for ru in range(2):
            for x in range(WW):
                table[i * 128 + ru * 64 + x, (ru * 2 + x % 2) * 128 + i * 32 + x // 2] = 1.0
    return table


def dot(a, b, dims=((1,), (0,)), precision=None):
    return lax.dot_general(a, b, (dims, ((), ())), preferred_element_type=F32, precision=precision)


NT = ((1,), (1,))


def plane_offsets():
    return [66 - 32 * ru - rv for ru in (1, 0) for rv in (1, 0)]


def split_planes(video, table):
    blocks = [video[:, t * 512 : (t + 1) * 512] for t in range(4)]
    tail = jnp.concatenate([video[:, 2048:2304], jnp.zeros((16, 256), BF16)], axis=1)
    stacked = jnp.concatenate(blocks + [tail], axis=0)
    split = dot(stacked, table)
    out = []
    for plane, offset in enumerate(plane_offsets()):
        parts = [split[t * 16 : (t + 1) * 16, plane * 128 : (plane + 1) * 128] for t in range(5)]
        flat = jnp.concatenate(parts + [jnp.zeros((16, 128), F32)], axis=1)
        out.append(pltpu.roll(flat, offset, 1))
    return out[::-1]


def column_masks():
    row = lax.broadcasted_iota(jnp.int32, (ROWS, POOLED), 0)
    column = lax.broadcasted_iota(jnp.int32, (ROWS, POOLED), 1) % 32
    masks = []
    for shift in range(4):
        at = column + shift - 2 + row % 2
        masks.append((at >= 0) & (at < 32) & (row < 12))
    return masks


def fill_patches(base, patches_ref, k, masks):
    for qu in range(4):
        for qv in range(4):
            shift = qu * 32 + qv
            moved = base if shift == 0 else pltpu.roll(base, BASE_W - shift, 1)
            tile = jnp.where(masks[qv], moved[:, :POOLED], 0.0)
            if shift == 0:
                row = lax.broadcasted_iota(jnp.int32, (ROWS, POOLED), 0)
                tile = jnp.where(row == 12, 1.0, tile)
            at = (qu * 4 + qv) * ROWS
            patches_ref[k, at : at + ROWS, :] = tile.astype(BF16)


def conv_matrix(conv_weight, fold_ref, w2_ref):
    for ab in range(4):
        block = dot(conv_weight, fold_ref[ab][:, :TAPS], NT)
        w2_ref[ab * CH : (ab + 1) * CH, :] = block.astype(BF16)


def remote(src, dst, sends, recvs, send_at, recv_at, peer):
    return pltpu.make_async_remote_copy(
        src_ref=src, dst_ref=dst, send_sem=sends.at[send_at], recv_sem=recvs.at[recv_at],
        device_id=peer, device_id_type=MESH,
    )


def iotas(shape):
    return lax.broadcasted_iota(jnp.int32, shape, 0), lax.broadcasted_iota(jnp.int32, shape, 1)


def one_hot(condition):
    return jnp.where(condition, 1.0, 0.0)


def sorting_matrix(assignment):
    row, _ = iotas((16, 16))
    pick = one_hot(assignment == row)
    row, col = iotas((16, 256))
    wide = dot(pick, one_hot(col % 16 == row))
    row, col = iotas((256, 16))
    tall = dot(one_hot(row // 16 == col), wide)
    row, col = iotas((256, 256))
    return jnp.where(row % 16 == col // 16, tall, 0.0).astype(BF16)


def column(line):
    row, col = iotas((CH, CH))
    one = jnp.sum(jnp.where(row == col, line, 0.0), axis=1, keepdims=True)
    return jnp.concatenate([one] * 4, axis=0)


def block_diagonal(matrix):
    row, col = iotas((CH, 256))
    wide = dot(matrix.astype(BF16), one_hot(col % CH == row).astype(BF16))
    row, col = iotas((256, 256))
    return jnp.where(row // CH == col // CH, jnp.concatenate([wide] * 4, axis=0), 0.0).astype(BF16)


def elu(values):
    return jnp.maximum(values, jnp.exp(jnp.minimum(values, 0.0)) - 1.0)


def finish_small(gmix_ref, gconv_ref, gbias_ref, fold_ref, loss):
    row, col = iotas((256, 256))
    total = jnp.zeros((CH, 256), F32)
    bias = jnp.sum(gbias_ref[...], axis=1, keepdims=True)
    for ab in range(4):
        rows = slice(ab * CH, (ab + 1) * CH)
        place = one_hot((row // CH == ab) & (col == row % CH + TAPS + 1))
        total += dot(gconv_ref[rows, :], fold_ref[ab].astype(F32), precision=lax.Precision.HIGHEST)
        total += dot(gmix_ref[rows, :], place, precision=lax.Precision.HIGHEST)
    line, lane = iotas((CH, 256))
    total = jnp.where(lane == TAPS + 1 + CH, bias, total)
    return jnp.where((lane == TAPS + 2 + CH) & (line == 0), loss, total)


def step_kernel(
    loss_scale,
    count_ref, video_ref, responses_ref, assign_ref, weight_ref, bias1_ref, mix_ref, bias2_ref,
    masks_hbm, featw_hbm, rbias_ref, table_ref, fold_ref,
    small_out, grads_out,
    mask_ref, featw_ref, planes_ref, prev_ref, after_ref, base_ref, w2_ref, mix4_ref, mixt_ref,
    patches_ref, act_ref, feats_ref, psend_ref, precv_ref, tsend_ref, trecv_ref, target_ref,
    turned_ref, proj_ref, mixed_ref, total_ref, loss_ref,
    blocks_ref, got_ref, half_ref, low_ref, up_ref, minus_low_ref, minus_high_ref, plus_low_ref, plus_high_ref, bsend_ref, brecv_ref,
    gmix_ref, gconv_ref, gmixb_ref, ar_ref, r1_ref, s2_ref, r2_ref, s3_ref, r3_ref,
    local_sem, halo_s, halo_r, pool_s, pool_r, targ_s, targ_r, pair_s, pair_r, ring_s, ring_r,
    back_s, back_r, a1_s, a1_r, a2_s, a2_r, a3_s, a3_r,
):
    sess = lax.axis_index("sess")
    clip = lax.axis_index("clip")
    row_y = clip // 2
    core = clip % 2

    mask_copy = pltpu.make_async_copy(masks_hbm.at[0], mask_ref, local_sem.at[0])
    featw_copy = pltpu.make_async_copy(featw_hbm.at[0], featw_ref, local_sem.at[1])
    mask_copy.start()
    featw_copy.start()

    barrier = pltpu.get_barrier_semaphore()

    def greet_sess(j, carry):
        pl.semaphore_signal(barrier, inc=1, device_id={"sess": (sess + j) % 16}, device_id_type=MESH)
        return carry

    def greet_clip(j, carry):
        pl.semaphore_signal(barrier, inc=1, device_id={"clip": (clip + j) % 8}, device_id_type=MESH)
        return carry

    lax.fori_loop(1, 16, greet_sess, 0)
    lax.fori_loop(1, 8, greet_clip, 0)

    planes = split_planes(video_ref[...], table_ref[...])
    planes_ref[...] = jnp.concatenate(planes, axis=0).astype(BF16)
    pl.semaphore_wait(barrier, 22)

    halo_up = remote(planes_ref, prev_ref, halo_s, halo_r, 0, 0, {"sess": (sess + 1) % 16})
    halo_down = remote(planes_ref, after_ref, halo_s, halo_r, 1, 1, {"sess": (sess + 15) % 16})
    halo_up.start()
    halo_down.start()

    sort = sorting_matrix(assign_ref[...])
    stacked = jnp.concatenate([responses_ref[:, q * 256 : (q + 1) * 256] for q in range(16)], axis=0)
    tsend_ref[...] = dot(sort, stacked).astype(BF16).reshape(16, 16, 256)

    def target_copy(j):
        peer = (sess + 1 + j) % 16
        return remote(tsend_ref.at[peer], trecv_ref.at[sess], targ_s, targ_r, peer, sess, {"sess": peer})

    def start_target(j, carry):
        target_copy(j).start()
        return carry

    lax.fori_loop(0, 15, start_target, 0)
    trecv_ref[sess] = tsend_ref[sess]

    conv_matrix(weight_ref[...], fold_ref, w2_ref)
    mix = mix_ref[...].astype(F32)
    mix4_ref[...] = block_diagonal(mix)
    mixt_ref[...] = block_diagonal(mix.T)
    bias1 = column(bias1_ref[...])
    bias2 = column(bias2_ref[...])
    masks = column_masks()

    halo_up.wait()
    halo_down.wait()
    none = jnp.zeros((64, BASE_W), BF16)
    prev = jnp.where(sess == 0, none, prev_ref[...])
    after = jnp.where(sess == 15, none, after_ref[...])
    window = jnp.concatenate([prev, planes_ref[...], after], axis=0)
    base_ref[...] = dot(sort[:, :192], window)

    def pooled_copy(j):
        peer = (sess + 1 + j) % 16
        return remote(psend_ref.at[peer], precv_ref.at[sess], pool_s, pool_r, peer, sess, {"sess": peer})

    def forward(i, carry):
        steps = [i * GROUP + g for g in range(GROUP)]
        clips = [(sess + 1 + j) % 16 for j in steps]
        for k in clips:
            fill_patches(base_ref[pl.ds(pl.multiple_of(k * ROWS, ROWS), ROWS), :], patches_ref, k, masks)
        pre1 = [dot(w2_ref[...], patches_ref[k]) for k in clips]
        act1 = [elu(p + bias1).astype(BF16) for p in pre1]
        pre2 = [dot(mix4_ref[...], a) for a in act1]
        feats = [elu(p + bias2).astype(BF16) for p in pre2]
        for k, a, f in zip(clips, act1, feats):
            act_ref[k] = a
            feats_ref[k] = f
            wide = f.astype(F32)
            total = (wide[0:64] + wide[64:128]) + (wide[128:192] + wide[192:256])
            psend_ref[k] = (total * 0.25).astype(BF16)
        for j in steps:

            @pl.when(j < 15)
            def _():
                pooled_copy(j).start()

        return carry

    lax.fori_loop(0, 16 // GROUP, forward, 0)
    precv_ref[sess] = psend_ref[sess]
    total_ref[...] = jnp.zeros_like(total_ref)
    loss_ref[...] = jnp.zeros_like(loss_ref)
    gmix_ref[...] = jnp.zeros_like(gmix_ref)
    gconv_ref[...] = jnp.zeros_like(gconv_ref)
    gmixb_ref[...] = jnp.zeros_like(gmixb_ref)
    mask_copy.wait()
    featw_copy.wait()

    def wait_forward(j, carry):
        peer = (sess + 15 - j) % 16
        there = (sess + 1 + j) % 16
        remote(psend_ref.at[there], precv_ref.at[peer], pool_s, pool_r, there, peer, {"sess": there}).wait()
        remote(tsend_ref.at[there], trecv_ref.at[peer], targ_s, targ_r, there, peer, {"sess": there}).wait()
        return carry

    lax.fori_loop(0, 15, wait_forward, 0)

    row, col = iotas((256, 256))
    swap = one_hot((row // 16 == col % 16) & (row % 16 == col // 16)).astype(BF16)
    target_ref[...] = dot(swap, trecv_ref[...].reshape(256, 256))
    turned_ref[...] = precv_ref[...].reshape(1024, POOLED).T

    partner = {"clip": row_y * 2 + 1 - core}
    right = {"clip": (row_y + 1) % 4 * 2 + core}
    left = {"clip": (row_y + 3) % 4 * 2 + core}
    high = GROWS - LOW

    def pair_copy(t):
        return remote(blocks_ref.at[t], got_ref.at[t], pair_s, pair_r, t, t, partner)

    def ring_copy(src, dst, at, peer):
        return remote(src, dst, ring_s, ring_r, at, at, peer)

    def lows(ref):
        return ref.at[pl.ds(0, LOW)]

    def highs(ref):
        return ref.at[pl.ds(LOW, high)]

    at_two = 4 + (row_y + 2) % 4
    at_one = 4 + (row_y + 1) % 4
    at_three = 4 + (row_y + 3) % 4
    relay_low = ring_copy(lows(half_ref.at[0]), low_ref, 0, right)
    relay_high = ring_copy(highs(half_ref.at[0]), up_ref, 1, left)
    right_high = ring_copy(highs(half_ref.at[1]), minus_high_ref, 2, right)
    left_low = ring_copy(lows(half_ref.at[1]), plus_low_ref, 3, left)
    right_low = ring_copy(lows(blocks_ref.at[at_one]), minus_low_ref, 4, right)
    left_high = ring_copy(highs(blocks_ref.at[at_three]), plus_high_ref, 5, left)

    def readout(slot, n):
        at = pl.ds(pl.multiple_of(n * NBLOCK, NBLOCK), NBLOCK)
        mask = mask_ref[:, at]
        weight = featw_ref[:, at].astype(F32)
        proj_ref[...] = dot(precv_ref[...].reshape(1024, POOLED), mask)
        drives = []
        for f in range(16):
            drives.append(jnp.sum(proj_ref[f * CH : (f + 1) * CH, :] * weight, axis=0, keepdims=True))
        drive = jnp.concatenate(drives, axis=0) + rbias_ref[:, at]
        first = target_ref[pl.ds(pl.multiple_of(n * 32, 32), 16), :]
        second = target_ref[pl.ds(pl.multiple_of(n * 32 + 16, 16), 16), :]
        target = jnp.concatenate([first, second], axis=1)
        small = jnp.exp(-jnp.abs(drive))
        rate = jnp.maximum(drive, 0.0) + jnp.log1p(small) + 0.1
        sigmoid = jnp.where(drive >= 0, 1.0, small) / (1.0 + small)
        place = n * NBLOCK + lax.broadcasted_iota(jnp.int32, (16, NBLOCK), 1)
        alive = place < count_ref[0]
        terms = jnp.where(alive, rate - target * jnp.log(rate), 0.0)
        loss_ref[...] += jnp.sum(terms, keepdims=True) * loss_scale
        grad_drive = jnp.where(alive, (1.0 - target / rate) * sigmoid, 0.0) * loss_scale
        feat = jnp.zeros((CH, NBLOCK), F32)
        for f in range(16):
            line = grad_drive[f : f + 1, :]
            feat += line * proj_ref[f * CH : (f + 1) * CH, :]
            mixed_ref[f * CH : (f + 1) * CH, :] = (line * weight).astype(BF16)
        blocks_ref[slot, POOLED : POOLED + CH, :] = feat
        bias_grad = jnp.sum(grad_drive, axis=0, keepdims=True)
        blocks_ref[slot, POOLED + CH : GROWS, :] = jnp.broadcast_to(bias_grad, (GROWS - POOLED - CH, NBLOCK))
        mixed = mixed_ref[...]
        blocks_ref[slot, 0:POOLED, :] = dot(turned_ref[...], mixed)
        total_ref[...] += dot(mixed, mask, NT)

    def phase(i, carry):
        t = (row_y + jnp.where(i == 0, 2, jnp.where(i == 1, 1, jnp.where(i == 2, 3, 0)))) % 4

        def half(h, inner):
            readout(h * 4 + t, t * 2 + jnp.where(h == 0, 1 - core, core))

            @pl.when(h == 0)
            def _():
                pair_copy(t).start()

            return inner

        lax.fori_loop(0, 2, half, 0)
        pair_copy(t).wait()
        blocks_ref[4 + t] += got_ref[t]

        @pl.when(i == 0)
        def _():
            half_ref[0] = blocks_ref[at_two].astype(BF16)
            relay_low.start()
            relay_high.start()

        @pl.when(i == 1)
        def _():
            half_ref[1, LOW:GROWS, :] = blocks_ref[at_one, LOW:GROWS, :].astype(BF16)
            right_high.start()

        @pl.when(i == 2)
        def _():
            half_ref[1, 0:LOW, :] = blocks_ref[at_three, 0:LOW, :].astype(BF16)
            left_low.start()
            relay_low.wait()
            blocks_ref[at_one, 0:LOW, :] += low_ref[...].astype(F32)
            right_low.start()
            relay_high.wait()
            blocks_ref[at_three, LOW:GROWS, :] += up_ref[...].astype(F32)
            left_high.start()

        return carry

    lax.fori_loop(0, 4, phase, 0)

    def back_copy(j):
        peer = (sess + 1 + j) % 16
        return remote(bsend_ref.at[peer], brecv_ref.at[sess], back_s, back_r, peer, sess, {"sess": peer})

    def send_back(j, carry):
        f = (sess + 1 + j) % 16
        bsend_ref[f] = total_ref[pl.ds(pl.multiple_of(f * CH, CH), CH), :].astype(BF16)

        @pl.when(j < 15)
        def _():
            back_copy(j).start()

        return carry

    lax.fori_loop(0, 16, send_back, 0)
    brecv_ref[sess] = bsend_ref[sess]

    one_half = jnp.asarray(1.0, BF16)
    zero_half = jnp.asarray(0.0, BF16)

    def backward(i, carry):
        steps = [i * GROUP + g for g in range(GROUP)]
        clips = [(sess + 16 - m) % 16 for m in steps]
        for m, k in zip(steps, clips):

            @pl.when(m > 0)
            def _():
                there = (sess + m) % 16
                remote(bsend_ref.at[there], brecv_ref.at[k], back_s, back_r, there, k, {"sess": there}).wait()

        grads = [brecv_ref[k] * jnp.asarray(0.25, BF16) for k in clips]
        slopes = [one_half + jnp.minimum(feats_ref[k], zero_half) for k in clips]
        pre2_grad = [jnp.concatenate([g] * 4, axis=0) * s for g, s in zip(grads, slopes)]
        act1 = [act_ref[k] for k in clips]
        act1_grad = [dot(mixt_ref[...], p) for p in pre2_grad]
        gmix_ref[...] += sum(dot(p, a, NT) for p, a in zip(pre2_grad, act1))
        slopes = [(one_half + jnp.minimum(a, zero_half)).astype(F32) for a in act1]
        pre1_grad = [(g * s).astype(BF16) for g, s in zip(act1_grad, slopes)]
        wide = sum(p.astype(F32) for p in pre2_grad)
        gmixb_ref[...] += (wide[0:64] + wide[64:128]) + (wide[128:192] + wide[192:256])
        gconv_ref[...] += sum(dot(p, patches_ref[k], NT) for p, k in zip(pre1_grad, clips))
        return carry

    lax.fori_loop(0, 16 // GROUP, backward, 0)

    small = finish_small(gmix_ref, gconv_ref, gmixb_ref, fold_ref, loss_ref[...])
    for piece in range(8):
        ar_ref[piece] = small[piece * 8 : piece * 8 + 8]

    def a1_copy(j, here):
        peer = (clip + 1 + j) % 8
        return remote(ar_ref.at[peer], r1_ref.at[here], a1_s, a1_r, peer, here, {"clip": peer})

    def a2_copy(j, here):
        peer = (sess + 1 + j) % 16
        return remote(s2_ref, r2_ref.at[here], a2_s, a2_r, peer, here, {"sess": peer})

    def a3_copy(j, here):
        peer = (clip + 1 + j) % 8
        return remote(s3_ref, r3_ref.at[here], a3_s, a3_r, peer, here, {"clip": peer})

    def begin_all(copy, count, mine):
        def begin(j, carry):
            copy(j, mine).start()
            return carry

        lax.fori_loop(0, count, begin, 0)

    def finish_all(copy, count, mine):
        def finish(j, carry):
            copy(j, (mine + count - j) % (count + 1)).wait()
            return carry

        lax.fori_loop(0, count, finish, 0)

    begin_all(a1_copy, 7, clip)
    r1_ref[clip] = ar_ref[clip]
    finish_all(a1_copy, 7, clip)
    part = jnp.sum(r1_ref[...], axis=0)
    s2_ref[...] = part
    begin_all(a2_copy, 15, sess)
    r2_ref[sess] = part
    finish_all(a2_copy, 15, sess)
    part = jnp.sum(r2_ref[...], axis=0)
    s3_ref[...] = part
    begin_all(a3_copy, 7, clip)
    r3_ref[clip] = part
    right_high.wait()
    left_low.wait()
    right_low.wait()
    left_high.wait()
    low = blocks_ref[4 + row_y, 0:LOW, :] + minus_low_ref[...]
    grads_out[0:LOW, :] = low + plus_low_ref[...].astype(F32)
    top = blocks_ref[4 + row_y, LOW:GROWS, :] + plus_high_ref[...]
    grads_out[LOW:GROWS, :] = top + minus_high_ref[...].astype(F32)
    finish_all(a3_copy, 7, clip)
    small_out[...] = r3_ref[...].reshape(CH, 256)


def split_kernel(
    small_ref, grads_ref, loss_out, conv_out, convb_out, mix_out, mixb_out, gmask_out, gfeat_out, gbias_out
):
    small = small_ref[...]
    conv_out[...] = small[:, :TAPS]
    row, col = iotas((CH, CH))
    convb_out[...] = jnp.sum(jnp.where(row == col, small[:, TAPS : TAPS + 1], 0.0), axis=0, keepdims=True)
    mix_out[...] = small[:, TAPS + 1 : TAPS + 1 + CH]
    mixb = small[:, TAPS + 1 + CH : TAPS + 2 + CH]
    mixb_out[...] = jnp.sum(jnp.where(row == col, mixb, 0.0), axis=0, keepdims=True)
    loss_out[...] = small[0:1, TAPS + 2 + CH : TAPS + 3 + CH]
    gmask_out[...] = grads_ref[0:POOLED]
    gfeat_out[...] = grads_ref[POOLED : POOLED + CH]
    gbias_out[...] = grads_ref[POOLED + CH : POOLED + CH + 1]


def run_split(small, grads):
    outs = [(1, 1), (CH, TAPS), (1, CH), (CH, CH), (1, CH), (POOLED, NBLOCK), (CH, NBLOCK), (1, NBLOCK)]
    return pl.pallas_call(
        split_kernel,
        out_shape=[jax.ShapeDtypeStruct(shape, F32) for shape in outs],
        name="split_results",
    )(small, grads)


def run_step(loss_scale, *args):
    def vmem(shape, dtype):
        return pltpu.VMEM(shape, dtype)

    def dma(n):
        return pltpu.SemaphoreType.DMA((n,))

    whole = pl.BlockSpec(memory_space=pltpu.VMEM)
    anywhere = pl.BlockSpec(memory_space=pl.ANY)
    smem = pl.BlockSpec(memory_space=pltpu.SMEM)
    outs = [(CH, 256), (GROWS, NBLOCK)]
    neurons = args[8].shape[2]
    return pl.pallas_call(
        functools.partial(step_kernel, loss_scale),
        in_specs=[smem] + [whole] * 7 + [anywhere] * 2 + [whole] * 3,
        out_specs=[whole] * 2,
        out_shape=[jax.ShapeDtypeStruct(shape, F32) for shape in outs],
        scratch_shapes=[
            vmem((POOLED, neurons), BF16),
            vmem((CH, neurons), BF16),
            vmem((64, BASE_W), BF16),
            vmem((64, BASE_W), BF16),
            vmem((64, BASE_W), BF16),
            vmem((256, BASE_W), F32),
            vmem((256, 256), BF16),
            vmem((256, 256), BF16),
            vmem((256, 256), BF16),
            vmem((16, 256, POOLED), BF16),
            vmem((16, 256, POOLED), BF16),
            vmem((16, 256, POOLED), BF16),
            vmem((16, CH, POOLED), BF16),
            vmem((16, CH, POOLED), BF16),
            vmem((16, 16, 256), BF16),
            vmem((16, 16, 256), BF16),
            vmem((256, 256), F32),
            vmem((POOLED, 1024), BF16),
            vmem((1024, NBLOCK), F32),
            vmem((1024, NBLOCK), BF16),
            vmem((1024, POOLED), F32),
            vmem((1, 1), F32),
            vmem((8, GROWS, NBLOCK), F32),
            vmem((4, GROWS, NBLOCK), F32),
            vmem((2, GROWS, NBLOCK), BF16),
            vmem((LOW, NBLOCK), BF16),
            vmem((GROWS - LOW, NBLOCK), BF16),
            vmem((LOW, NBLOCK), F32),
            vmem((GROWS - LOW, NBLOCK), BF16),
            vmem((LOW, NBLOCK), BF16),
            vmem((GROWS - LOW, NBLOCK), F32),
            vmem((16, CH, POOLED), BF16),
            vmem((16, CH, POOLED), BF16),
            vmem((256, 256), F32),
            vmem((256, 256), F32),
            vmem((CH, POOLED), F32),
            vmem((8, 8, 256), F32),
            vmem((8, 8, 256), F32),
            vmem((8, 256), F32),
            vmem((16, 8, 256), F32),
            vmem((8, 256), F32),
            vmem((8, 8, 256), F32),
        ]
        + [dma(n) for n in (2, 2, 2, 16, 16, 16, 16, 4, 4, 6, 6, 16, 16, 8, 8, 16, 16, 8, 8)],
        compiler_params=pltpu.CompilerParams(
            collective_id=0, has_side_effects=True, vmem_limit_bytes=VM
        ),
        name="train_step",
    )(*args)


def per_device(
    video, responses, assignment, counts, conv_weight, conv_bias, mix_weight, mix_bias, masks, feat_w, readout_bias,
):
    sess_total = lax.axis_size("sess")
    clip_total = lax.axis_size("clip")
    loss_scale = 1.0 / (video.shape[0] * clip_total * sess_total)
    small, grads = run_step(
        loss_scale,
        counts,
        video.reshape(video.shape[0], -1),
        responses.reshape(responses.shape[0], -1),
        assignment[None],
        conv_weight,
        conv_bias[None],
        mix_weight,
        mix_bias[None],
        jnp.swapaxes(masks, 1, 2),
        jnp.swapaxes(feat_w, 1, 2),
        readout_bias,
        jnp.asarray(split_table(), BF16),
        jnp.asarray(tap_tables(), BF16),
    )
    loss, gconv, gconvb, gmix, gmixb, gmask, gfeat, gbias = run_split(small, grads)
    return (
        loss[0, 0],
        gconv,
        gconvb[0],
        gmix,
        gmixb[0],
        gmask.T[None],
        gfeat.T[None],
        gbias,
    )


def solution(mesh):
    return jax.shard_map(
        per_device,
        mesh=mesh,
        in_specs=(
            P("clip", "sess", None),
            P("clip", "sess", None),
            P("clip"),
            P("sess"),
            P(),
            P(),
            P(),
            P(),
            P("sess", None, None),
            P("sess", None, None),
            P("sess", None),
        ),
        out_specs=(
            P(),
            P(),
            P(),
            P(),
            P(),
            P("sess", "clip", None),
            P("sess", "clip", None),
            P("sess", "clip"),
        ),
        check_vma=False,
    )
```

```python
import functools

import jax
import jax.numpy as jnp
import numpy as np
from jax import lax
from jax.experimental import pallas as pl
from jax.experimental.pallas import tpu as pltpu
from jax.sharding import PartitionSpec as P

HH = 36
WW = 64
KS = 7
KT = 3
CH = 64
POOLED = 576
TAPS = 147
BASE_W = 768
ROWS = 16
NBLOCK = 512
GROWS = 656
F32 = jnp.float32
BF16 = jnp.bfloat16
VM = 60 * 2**20
LOW = 336
GROUP = 2
HALF = 8
RELAY_AT = 2
MESH = pl.DeviceIdType.MESH


def tap_tables():
    fold = np.zeros((4, 256, 256), np.float32)
    for a in range(2):
        for b in range(2):
            for dt in range(KT):
                for dy in range(KS):
                    for dx in range(KS):
                        u, v = dy + a, dx + b
                        depth = ((u // 2) * 4 + v // 2) * ROWS + dt * 4 + (u % 2) * 2 + v % 2
                        fold[a * 2 + b, depth, (dt * KS + dy) * KS + dx] = 1.0
            fold[a * 2 + b, 12, TAPS] = 1.0
    return fold


def split_table():
    table = np.zeros((512, 512), np.float32)
    for i in range(4):
        for ru in range(2):
            for x in range(WW):
                table[i * 128 + ru * 64 + x, (ru * 2 + x % 2) * 128 + i * 32 + x // 2] = 1.0
    return table


def dot(a, b, dims=((1,), (0,)), precision=None):
    return lax.dot_general(a, b, (dims, ((), ())), preferred_element_type=F32, precision=precision)


NT = ((1,), (1,))


def plane_offsets():
    return [66 - 32 * ru - rv for ru in (1, 0) for rv in (1, 0)]


def split_planes(video, table):
    blocks = [video[:, t * 512 : (t + 1) * 512] for t in range(4)]
    tail = jnp.concatenate([video[:, 2048:2304], jnp.zeros((16, 256), BF16)], axis=1)
    stacked = jnp.concatenate(blocks + [tail], axis=0)
    split = dot(stacked, table)
    out = []
    for plane, offset in enumerate(plane_offsets()):
        parts = [split[t * 16 : (t + 1) * 16, plane * 128 : (plane + 1) * 128] for t in range(5)]
        flat = jnp.concatenate(parts + [jnp.zeros((16, 128), F32)], axis=1)
        out.append(pltpu.roll(flat, offset, 1))
    return out[::-1]


def column_masks():
    row = lax.broadcasted_iota(jnp.int32, (ROWS, POOLED), 0)
    column = lax.broadcasted_iota(jnp.int32, (ROWS, POOLED), 1) % 32
    masks = []
    for shift in range(4):
        at = column + shift - 2 + row % 2
        masks.append((at >= 0) & (at < 32) & (row < 12))
    return masks


def fill_patches(base, patches_ref, k, masks):
    for qu in range(4):
        for qv in range(4):
            shift = qu * 32 + qv
            moved = base if shift == 0 else pltpu.roll(base, BASE_W - shift, 1)
            tile = jnp.where(masks[qv], moved[:, :POOLED], 0.0)
            if shift == 0:
                row = lax.broadcasted_iota(jnp.int32, (ROWS, POOLED), 0)
                tile = jnp.where(row == 12, 1.0, tile)
            at = (qu * 4 + qv) * ROWS
            patches_ref[k, at : at + ROWS, :] = tile.astype(BF16)


def conv_matrix(conv_weight, fold_ref, w2_ref):
    for ab in range(4):
        block = dot(conv_weight, fold_ref[ab][:, :TAPS], NT)
        w2_ref[ab * CH : (ab + 1) * CH, :] = block.astype(BF16)


def remote(src, dst, sends, recvs, send_at, recv_at, peer):
    return pltpu.make_async_remote_copy(
        src_ref=src, dst_ref=dst, send_sem=sends.at[send_at], recv_sem=recvs.at[recv_at],
        device_id=peer, device_id_type=MESH,
    )


def iotas(shape):
    return lax.broadcasted_iota(jnp.int32, shape, 0), lax.broadcasted_iota(jnp.int32, shape, 1)


def one_hot(condition):
    return jnp.where(condition, 1.0, 0.0)


def sorting_matrix(assignment):
    row, _ = iotas((16, 16))
    pick = one_hot(assignment == row)
    row, col = iotas((16, 256))
    wide = dot(pick, one_hot(col % 16 == row))
    row, col = iotas((256, 16))
    tall = dot(one_hot(row // 16 == col), wide)
    row, col = iotas((256, 256))
    return jnp.where(row % 16 == col // 16, tall, 0.0).astype(BF16)


def column(line):
    row, col = iotas((CH, CH))
    one = jnp.sum(jnp.where(row == col, line, 0.0), axis=1, keepdims=True)
    return jnp.concatenate([one] * 4, axis=0)


def block_diagonal(matrix):
    row, col = iotas((CH, 256))
    wide = dot(matrix.astype(BF16), one_hot(col % CH == row).astype(BF16))
    row, col = iotas((256, 256))
    return jnp.where(row // CH == col // CH, jnp.concatenate([wide] * 4, axis=0), 0.0).astype(BF16)


def elu(values):
    return jnp.maximum(values, jnp.exp(jnp.minimum(values, 0.0)) - 1.0)


def finish_small(gmix_ref, gconv_ref, gbias_ref, fold_ref, loss):
    row, col = iotas((256, 256))
    total = jnp.zeros((CH, 256), F32)
    bias = jnp.sum(gbias_ref[...], axis=1, keepdims=True)
    for ab in range(4):
        rows = slice(ab * CH, (ab + 1) * CH)
        place = one_hot((row // CH == ab) & (col == row % CH + TAPS + 1))
        total += dot(gconv_ref[rows, :], fold_ref[ab].astype(F32), precision=lax.Precision.HIGHEST)
        total += dot(gmix_ref[rows, :], place, precision=lax.Precision.HIGHEST)
    line, lane = iotas((CH, 256))
    total = jnp.where(lane == TAPS + 1 + CH, bias, total)
    return jnp.where((lane == TAPS + 2 + CH) & (line == 0), loss, total)


def step_kernel(
    loss_scale,
    count_ref, video_ref, responses_ref, assign_ref, weight_ref, bias1_ref, mix_ref, bias2_ref,
    masks_hbm, featw_hbm, rbias_ref, table_ref, fold_ref,
    small_out, grads_out,
    mask_ref, featw_ref, planes_ref, prev_ref, after_ref, base_ref, w2_ref, mix4_ref, mixt_ref,
    patches_ref, act_ref, feats_ref, psend_ref, precv_ref, tsend_ref, trecv_ref, target_ref,
    turned_ref, proj_ref, mixed_ref, total_ref, loss_ref,
    blocks_ref, got_ref, half_ref, low_ref, up_ref, minus_low_ref, minus_high_ref, plus_low_ref, plus_high_ref, bsend_ref, brecv_ref,
    gmix_ref, gconv_ref, gmixb_ref, ar_ref, r1_ref, s2_ref, r2_ref, s3_ref, r3_ref,
    local_sem, halo_s, halo_r, pool_s, pool_r, targ_s, targ_r, pair_s, pair_r, ring_s, ring_r,
    back_s, back_r, a1_s, a1_r, a2_s, a2_r, a3_s, a3_r,
):
    sess = lax.axis_index("sess")
    clip = lax.axis_index("clip")
    row_y = clip // 2
    core = clip % 2

    mask_copy = pltpu.make_async_copy(masks_hbm.at[0], mask_ref, local_sem.at[0])
    featw_copy = pltpu.make_async_copy(featw_hbm.at[0], featw_ref, local_sem.at[1])
    mask_copy.start()
    featw_copy.start()

    def shift(m):
        dz = m % 8 // 2
        return dz, m % 2 * 2 + (dz + m // 8) % 2

    def target_of(m):
        dz, dx = shift(m)
        return (sess // 4 + dz) % 4 * 4 + (sess + dx) % 4

    def source_of(m):
        dz, dx = shift(m)
        return (sess // 4 + 4 - dz) % 4 * 4 + (sess + 4 - dx) % 4

    barrier = pltpu.get_barrier_semaphore()

    def greet_sess(j, carry):
        pl.semaphore_signal(barrier, inc=1, device_id={"sess": (sess + j) % 16}, device_id_type=MESH)
        return carry

    def greet_clip(j, carry):
        pl.semaphore_signal(barrier, inc=1, device_id={"clip": (clip + j) % 8}, device_id_type=MESH)
        return carry

    lax.fori_loop(1, 16, greet_sess, 0)
    lax.fori_loop(1, 8, greet_clip, 0)

    planes = split_planes(video_ref[...], table_ref[...])
    planes_ref[...] = jnp.concatenate(planes, axis=0).astype(BF16)
    pl.semaphore_wait(barrier, 22)

    halo_up = remote(planes_ref, prev_ref, halo_s, halo_r, 0, 0, {"sess": (sess + 1) % 16})
    halo_down = remote(planes_ref, after_ref, halo_s, halo_r, 1, 1, {"sess": (sess + 15) % 16})
    halo_up.start()
    halo_down.start()

    sort = sorting_matrix(assign_ref[...])
    stacked = jnp.concatenate([responses_ref[:, q * 256 : (q + 1) * 256] for q in range(16)], axis=0)
    tsend_ref[...] = dot(sort, stacked).astype(BF16).reshape(16, 16, 256)

    def target_copy(m):
        peer = target_of(m)
        return remote(tsend_ref.at[peer], trecv_ref.at[m], targ_s, targ_r, m, m, {"sess": peer})

    def start_target(m, carry):
        target_copy(m).start()
        return carry

    lax.fori_loop(1, 16, start_target, 0)
    trecv_ref[0] = tsend_ref[sess]

    conv_matrix(weight_ref[...], fold_ref, w2_ref)
    mix = mix_ref[...].astype(F32)
    mix4_ref[...] = block_diagonal(mix)
    mixt_ref[...] = block_diagonal(mix.T)
    bias1 = column(bias1_ref[...])
    bias2 = column(bias2_ref[...])
    masks = column_masks()

    halo_up.wait()
    halo_down.wait()
    none = jnp.zeros((64, BASE_W), BF16)
    prev = jnp.where(sess == 0, none, prev_ref[...])
    after = jnp.where(sess == 15, none, after_ref[...])
    window = jnp.concatenate([prev, planes_ref[...], after], axis=0)
    base_ref[...] = dot(sort[:, :192], window)

    def pooled_copy(m):
        peer = target_of(m)
        return remote(psend_ref.at[peer], precv_ref.at[m], pool_s, pool_r, m, m, {"sess": peer})

    def forward(i, carry):
        steps = [i * GROUP + g for g in range(GROUP)]
        clips = [target_of((j + 1) % 16) for j in steps]
        for k in clips:
            fill_patches(base_ref[pl.ds(pl.multiple_of(k * ROWS, ROWS), ROWS), :], patches_ref, k, masks)
        pre1 = [dot(w2_ref[...], patches_ref[k]) for k in clips]
        act1 = [elu(p + bias1).astype(BF16) for p in pre1]
        pre2 = [dot(mix4_ref[...], a) for a in act1]
        feats = [elu(p + bias2).astype(BF16) for p in pre2]
        for k, a, f in zip(clips, act1, feats):
            act_ref[k] = a
            feats_ref[k] = f
            wide = f.astype(F32)
            total = (wide[0:64] + wide[64:128]) + (wide[128:192] + wide[192:256])
            psend_ref[k] = (total * 0.25).astype(BF16)
        for j in steps:

            @pl.when(j < 15)
            def _():
                pooled_copy(j + 1).start()

        return carry

    lax.fori_loop(0, 16 // GROUP, forward, 0)
    precv_ref[0] = psend_ref[sess]
    total_ref[...] = jnp.zeros_like(total_ref)
    loss_ref[...] = jnp.zeros_like(loss_ref)
    gmix_ref[...] = jnp.zeros_like(gmix_ref)
    gconv_ref[...] = jnp.zeros_like(gconv_ref)
    gmixb_ref[...] = jnp.zeros_like(gmixb_ref)
    mask_copy.wait()
    featw_copy.wait()

    def wait_pooled(m, carry):
        pooled_copy(m).wait()
        return carry

    def wait_target(m, carry):
        target_copy(m).wait()
        return carry

    lax.fori_loop(1, 16, wait_target, 0)
    row, col = iotas((256, 256))
    swap = one_hot((row // 16 == col % 16) & (row % 16 == col // 16)).astype(BF16)
    target_ref[...] = dot(swap, trecv_ref[...].reshape(256, 256))

    partner = {"clip": row_y * 2 + 1 - core}
    right = {"clip": (row_y + 1) % 4 * 2 + core}
    left = {"clip": (row_y + 3) % 4 * 2 + core}
    high = GROWS - LOW

    def pair_copy(t):
        return remote(blocks_ref.at[t], got_ref.at[t], pair_s, pair_r, t, t, partner)

    def ring_copy(src, dst, at, peer):
        return remote(src, dst, ring_s, ring_r, at, at, peer)

    def lows(ref):
        return ref.at[pl.ds(0, LOW)]

    def highs(ref):
        return ref.at[pl.ds(LOW, high)]

    at_two = 4 + (row_y + 2) % 4
    at_one = 4 + (row_y + 1) % 4
    at_three = 4 + (row_y + 3) % 4
    relay_low = ring_copy(lows(half_ref.at[0]), low_ref, 0, right)
    relay_high = ring_copy(highs(half_ref.at[0]), up_ref, 1, left)
    right_high = ring_copy(highs(half_ref.at[1]), minus_high_ref, 2, right)
    left_low = ring_copy(lows(half_ref.at[1]), plus_low_ref, 3, left)
    right_low = ring_copy(lows(blocks_ref.at[at_one]), minus_low_ref, 4, right)
    left_high = ring_copy(highs(blocks_ref.at[at_three]), plus_high_ref, 5, left)

    def readout(slot, n, half):
        at = pl.ds(pl.multiple_of(n * NBLOCK, NBLOCK), NBLOCK)
        frames = slice(half * HALF, (half + 1) * HALF)
        rows = slice(half * HALF * CH, (half + 1) * HALF * CH)
        mask = mask_ref[:, at]
        weight = featw_ref[:, at].astype(F32)
        proj_ref[...] = dot(precv_ref[frames].reshape(HALF * CH, POOLED), mask)
        drives = []
        for f in range(HALF):
            drives.append(jnp.sum(proj_ref[f * CH : (f + 1) * CH, :] * weight, axis=0, keepdims=True))
        drive = jnp.concatenate(drives, axis=0) + rbias_ref[:, at]
        first = target_ref[pl.ds(pl.multiple_of(n * 32 + half * HALF, HALF), HALF), :]
        second = target_ref[pl.ds(pl.multiple_of(n * 32 + 16 + half * HALF, HALF), HALF), :]
        target = jnp.concatenate([first, second], axis=1)
        small = jnp.exp(-jnp.abs(drive))
        rate = jnp.maximum(drive, 0.0) + jnp.log1p(small) + 0.1
        sigmoid = jnp.where(drive >= 0, 1.0, small) / (1.0 + small)
        place = n * NBLOCK + lax.broadcasted_iota(jnp.int32, (HALF, NBLOCK), 1)
        alive = place < count_ref[0]
        terms = jnp.where(alive, rate - target * jnp.log(rate), 0.0)
        loss_ref[...] += jnp.sum(terms, keepdims=True) * loss_scale
        grad_drive = jnp.where(alive, (1.0 - target / rate) * sigmoid, 0.0) * loss_scale
        feat = jnp.zeros((CH, NBLOCK), F32)
        for f in range(HALF):
            line = grad_drive[f : f + 1, :]
            feat += line * proj_ref[f * CH : (f + 1) * CH, :]
            mixed_ref[f * CH : (f + 1) * CH, :] = (line * weight).astype(BF16)
        bias_grad = jnp.sum(grad_drive, axis=0, keepdims=True)
        bias_grad = jnp.broadcast_to(bias_grad, (GROWS - POOLED - CH, NBLOCK))
        mixed = mixed_ref[...]
        mask_grad = dot(turned_ref[...], mixed)
        if half == 0:
            blocks_ref[slot, 0:POOLED, :] = mask_grad
            blocks_ref[slot, POOLED : POOLED + CH, :] = feat
            blocks_ref[slot, POOLED + CH : GROWS, :] = bias_grad
        else:
            blocks_ref[slot, 0:POOLED, :] += mask_grad
            blocks_ref[slot, POOLED : POOLED + CH, :] += feat
            blocks_ref[slot, POOLED + CH : GROWS, :] += bias_grad
        total_ref[rows, :] += dot(mixed, mask, NT)

    def back_copy(m):
        peer = source_of(m)
        return remote(bsend_ref.at[m], brecv_ref.at[m], back_s, back_r, m, m, {"sess": peer})

    def send_back(m, carry):
        bsend_ref[m] = total_ref[pl.ds(pl.multiple_of(m * CH, CH), CH), :].astype(BF16)

        @pl.when(m > 0)
        def _():
            back_copy(m).start()

        return carry

    def first_pass(i, carry):
        t, h = i // 2, i % 2
        readout(h * 4 + t, t * 2 + jnp.where(h == 0, 1 - core, core), 0)
        return carry

    lax.fori_loop(1, HALF, wait_pooled, 0)
    turned_ref[...] = precv_ref[0:HALF].reshape(HALF * CH, POOLED).T
    lax.fori_loop(0, 8, first_pass, 0)
    lax.fori_loop(0, HALF, send_back, 0)
    brecv_ref[0] = bsend_ref[0]
    lax.fori_loop(HALF, 16, wait_pooled, 0)
    turned_ref[...] = precv_ref[HALF:16].reshape(HALF * CH, POOLED).T

    def turn_of(i):
        return (row_y + jnp.where(i == 0, 2, jnp.where(i == 1, 1, jnp.where(i == 2, 3, 0)))) % 4

    def take_pair(t):
        pair_copy(t).wait()
        blocks_ref[4 + t] += got_ref[t]

    def phase(i, carry):
        t = turn_of(i)

        def half(h, inner):
            readout(h * 4 + t, t * 2 + jnp.where(h == 0, 1 - core, core), 1)

            @pl.when(h == 0)
            def _():
                pair_copy(t).start()

            return inner

        lax.fori_loop(0, 2, half, 0)

        @pl.when(i > 0)
        def _():
            take_pair(turn_of(i - 1))

        @pl.when(i == 1)
        def _():
            half_ref[0] = blocks_ref[at_two].astype(BF16)
            relay_low.start()
            relay_high.start()

        @pl.when(i == 2)
        def _():
            half_ref[1, LOW:GROWS, :] = blocks_ref[at_one, LOW:GROWS, :].astype(BF16)
            right_high.start()

        @pl.when(i == 3)
        def _():
            half_ref[1, 0:LOW, :] = blocks_ref[at_three, 0:LOW, :].astype(BF16)
            left_low.start()

        return carry

    lax.fori_loop(0, 4, phase, 0)
    lax.fori_loop(HALF, 16, send_back, 0)

    one_half = jnp.asarray(1.0, BF16)
    zero_half = jnp.asarray(0.0, BF16)

    def backward(i, carry):
        steps = [i * GROUP + g for g in range(GROUP)]
        clips = [target_of(m) for m in steps]

        @pl.when(i == RELAY_AT)
        def _():
            relay_low.wait()
            blocks_ref[at_one, 0:LOW, :] += low_ref[...].astype(F32)
            right_low.start()
            relay_high.wait()
            blocks_ref[at_three, LOW:GROWS, :] += up_ref[...].astype(F32)
            left_high.start()

        for m in steps:

            @pl.when(m > 0)
            def _():
                back_copy(m).wait()

        grads = [brecv_ref[m] * jnp.asarray(0.25, BF16) for m in steps]
        slopes = [one_half + jnp.minimum(feats_ref[k], zero_half) for k in clips]
        pre2_grad = [jnp.concatenate([g] * 4, axis=0) * s for g, s in zip(grads, slopes)]
        act1 = [act_ref[k] for k in clips]
        act1_grad = [dot(mixt_ref[...], p) for p in pre2_grad]
        gmix_ref[...] += sum(dot(p, a, NT) for p, a in zip(pre2_grad, act1))
        slopes = [(one_half + jnp.minimum(a, zero_half)).astype(F32) for a in act1]
        pre1_grad = [(g * s).astype(BF16) for g, s in zip(act1_grad, slopes)]
        wide = sum(p.astype(F32) for p in pre2_grad)
        gmixb_ref[...] += (wide[0:64] + wide[64:128]) + (wide[128:192] + wide[192:256])
        gconv_ref[...] += sum(dot(p, patches_ref[k], NT) for p, k in zip(pre1_grad, clips))
        return carry

    lax.fori_loop(0, 16 // GROUP, backward, 0)

    small = finish_small(gmix_ref, gconv_ref, gmixb_ref, fold_ref, loss_ref[...])
    for piece in range(16):
        top, lane = piece // 2 * 8, piece % 2 * 128
        ar_ref[piece] = small[top : top + 8, lane : lane + 128]

    def a1_copy(j, here):
        peer = (sess + 1 + j) % 16
        return remote(ar_ref.at[peer], r1_ref.at[here], a1_s, a1_r, peer, here, {"sess": peer})

    def a2_copy(j, here):
        peer = (clip + 1 + j) % 8
        return remote(s2_ref, r2_ref.at[here], a2_s, a2_r, peer, here, {"clip": peer})

    def a3_copy(j, here):
        peer = (sess + 1 + j) % 16
        return remote(s3_ref, r3_ref.at[here], a3_s, a3_r, peer, here, {"sess": peer})

    def begin_all(copy, count, mine):
        def begin(j, carry):
            copy(j, mine).start()
            return carry

        lax.fori_loop(0, count, begin, 0)

    def finish_all(copy, count, mine):
        def finish(j, carry):
            copy(j, (mine + count - j) % (count + 1)).wait()
            return carry

        lax.fori_loop(0, count, finish, 0)

    begin_all(a1_copy, 15, sess)
    r1_ref[sess] = ar_ref[sess]
    finish_all(a1_copy, 15, sess)
    part = jnp.sum(r1_ref[...], axis=0)
    s2_ref[...] = part
    begin_all(a2_copy, 7, clip)
    r2_ref[clip] = part
    finish_all(a2_copy, 7, clip)
    part = jnp.sum(r2_ref[...], axis=0)
    s3_ref[...] = part
    begin_all(a3_copy, 15, sess)
    r3_ref[sess] = part
    take_pair(row_y)
    right_high.wait()
    left_low.wait()
    right_low.wait()
    left_high.wait()
    low = blocks_ref[4 + row_y, 0:LOW, :] + minus_low_ref[...]
    grads_out[0:LOW, :] = low + plus_low_ref[...].astype(F32)
    top = blocks_ref[4 + row_y, LOW:GROWS, :] + plus_high_ref[...]
    grads_out[LOW:GROWS, :] = top + minus_high_ref[...].astype(F32)
    finish_all(a3_copy, 15, sess)
    lines = [jnp.concatenate([r3_ref[2 * r], r3_ref[2 * r + 1]], axis=1) for r in range(8)]
    small_out[...] = jnp.concatenate(lines, axis=0)


def split_kernel(
    small_ref, grads_ref, loss_out, conv_out, convb_out, mix_out, mixb_out, gmask_out, gfeat_out, gbias_out
):
    small = small_ref[...]
    conv_out[...] = small[:, :TAPS]
    row, col = iotas((CH, CH))
    convb_out[...] = jnp.sum(jnp.where(row == col, small[:, TAPS : TAPS + 1], 0.0), axis=0, keepdims=True)
    mix_out[...] = small[:, TAPS + 1 : TAPS + 1 + CH]
    mixb = small[:, TAPS + 1 + CH : TAPS + 2 + CH]
    mixb_out[...] = jnp.sum(jnp.where(row == col, mixb, 0.0), axis=0, keepdims=True)
    loss_out[...] = small[0:1, TAPS + 2 + CH : TAPS + 3 + CH]
    gmask_out[...] = grads_ref[0:POOLED]
    gfeat_out[...] = grads_ref[POOLED : POOLED + CH]
    gbias_out[...] = grads_ref[POOLED + CH : POOLED + CH + 1]


def run_split(small, grads):
    outs = [(1, 1), (CH, TAPS), (1, CH), (CH, CH), (1, CH), (POOLED, NBLOCK), (CH, NBLOCK), (1, NBLOCK)]
    return pl.pallas_call(
        split_kernel,
        out_shape=[jax.ShapeDtypeStruct(shape, F32) for shape in outs],
        name="split_results",
    )(small, grads)


def run_step(loss_scale, *args):
    def vmem(shape, dtype):
        return pltpu.VMEM(shape, dtype)

    def dma(n):
        return pltpu.SemaphoreType.DMA((n,))

    whole = pl.BlockSpec(memory_space=pltpu.VMEM)
    anywhere = pl.BlockSpec(memory_space=pl.ANY)
    smem = pl.BlockSpec(memory_space=pltpu.SMEM)
    outs = [(CH, 256), (GROWS, NBLOCK)]
    neurons = args[8].shape[2]
    return pl.pallas_call(
        functools.partial(step_kernel, loss_scale),
        in_specs=[smem] + [whole] * 7 + [anywhere] * 2 + [whole] * 3,
        out_specs=[whole] * 2,
        out_shape=[jax.ShapeDtypeStruct(shape, F32) for shape in outs],
        scratch_shapes=[
            vmem((POOLED, neurons), BF16),
            vmem((CH, neurons), BF16),
            vmem((64, BASE_W), BF16),
            vmem((64, BASE_W), BF16),
            vmem((64, BASE_W), BF16),
            vmem((256, BASE_W), F32),
            vmem((256, 256), BF16),
            vmem((256, 256), BF16),
            vmem((256, 256), BF16),
            vmem((16, 256, POOLED), BF16),
            vmem((16, 256, POOLED), BF16),
            vmem((16, 256, POOLED), BF16),
            vmem((16, CH, POOLED), BF16),
            vmem((16, CH, POOLED), BF16),
            vmem((16, 16, 256), BF16),
            vmem((16, 16, 256), BF16),
            vmem((256, 256), F32),
            vmem((POOLED, HALF * CH), BF16),
            vmem((HALF * CH, NBLOCK), F32),
            vmem((HALF * CH, NBLOCK), BF16),
            vmem((1024, POOLED), F32),
            vmem((1, 1), F32),
            vmem((8, GROWS, NBLOCK), F32),
            vmem((4, GROWS, NBLOCK), F32),
            vmem((2, GROWS, NBLOCK), BF16),
            vmem((LOW, NBLOCK), BF16),
            vmem((GROWS - LOW, NBLOCK), BF16),
            vmem((LOW, NBLOCK), F32),
            vmem((GROWS - LOW, NBLOCK), BF16),
            vmem((LOW, NBLOCK), BF16),
            vmem((GROWS - LOW, NBLOCK), F32),
            vmem((16, CH, POOLED), BF16),
            vmem((16, CH, POOLED), BF16),
            vmem((256, 256), F32),
            vmem((256, 256), F32),
            vmem((CH, POOLED), F32),
            vmem((16, 8, 128), F32),
            vmem((16, 8, 128), F32),
            vmem((8, 128), F32),
            vmem((8, 8, 128), F32),
            vmem((8, 128), F32),
            vmem((16, 8, 128), F32),
        ]
        + [dma(n) for n in (2, 2, 2, 16, 16, 16, 16, 4, 4, 6, 6, 16, 16, 16, 16, 8, 8, 16, 16)],
        compiler_params=pltpu.CompilerParams(
            collective_id=0, has_side_effects=True, vmem_limit_bytes=VM
        ),
        name="train_step",
    )(*args)


def per_device(
    video, responses, assignment, counts, conv_weight, conv_bias, mix_weight, mix_bias, masks, feat_w, readout_bias,
):
    sess_total = lax.axis_size("sess")
    clip_total = lax.axis_size("clip")
    loss_scale = 1.0 / (video.shape[0] * clip_total * sess_total)
    small, grads = run_step(
        loss_scale,
        counts,
        video.reshape(video.shape[0], -1),
        responses.reshape(responses.shape[0], -1),
        assignment[None],
        conv_weight,
        conv_bias[None],
        mix_weight,
        mix_bias[None],
        jnp.swapaxes(masks, 1, 2),
        jnp.swapaxes(feat_w, 1, 2),
        readout_bias,
        jnp.asarray(split_table(), BF16),
        jnp.asarray(tap_tables(), BF16),
    )
    loss, gconv, gconvb, gmix, gmixb, gmask, gfeat, gbias = run_split(small, grads)
    return (
        loss[0, 0],
        gconv,
        gconvb[0],
        gmix,
        gmixb[0],
        gmask.T[None],
        gfeat.T[None],
        gbias,
    )


def solution(mesh):
    return jax.shard_map(
        per_device,
        mesh=mesh,
        in_specs=(
            P("clip", "sess", None),
            P("clip", "sess", None),
            P("clip"),
            P("sess"),
            P(),
            P(),
            P(),
            P(),
            P("sess", None, None),
            P("sess", None, None),
            P("sess", None),
        ),
        out_specs=(
            P(),
            P(),
            P(),
            P(),
            P(),
            P("sess", "clip", None),
            P("sess", "clip", None),
            P("sess", "clip"),
        ),
        check_vma=False,
    )
```

```python
import functools

import jax
import jax.numpy as jnp
import numpy as np
from jax import lax
from jax.experimental import pallas as pl
from jax.experimental.pallas import tpu as pltpu
from jax.sharding import PartitionSpec as P

HH = 36
WW = 64
KS = 7
KT = 3
CH = 64
POOLED = 576
TAPS = 147
BASE_W = 768
ROWS = 16
NBLOCK = 512
GROWS = 656
F32 = jnp.float32
BF16 = jnp.bfloat16
VM = 60 * 2**20
LOW = 336
GROUP = 2
HALF = 8
RELAY_AT = 2
MESH = pl.DeviceIdType.MESH


def tap_tables():
    fold = np.zeros((4, 256, 256), np.float32)
    for a in range(2):
        for b in range(2):
            for dt in range(KT):
                for dy in range(KS):
                    for dx in range(KS):
                        u, v = dy + a, dx + b
                        depth = ((u // 2) * 4 + v // 2) * ROWS + dt * 4 + (u % 2) * 2 + v % 2
                        fold[a * 2 + b, depth, (dt * KS + dy) * KS + dx] = 1.0
            fold[a * 2 + b, 12, TAPS] = 1.0
    return fold


def split_table():
    table = np.zeros((512, 512), np.float32)
    for i in range(4):
        for ru in range(2):
            for x in range(WW):
                table[i * 128 + ru * 64 + x, (ru * 2 + x % 2) * 128 + i * 32 + x // 2] = 1.0
    return table


def dot(a, b, dims=((1,), (0,)), precision=None):
    return lax.dot_general(a, b, (dims, ((), ())), preferred_element_type=F32, precision=precision)


NT = ((1,), (1,))


def plane_offsets():
    return [66 - 32 * ru - rv for ru in (1, 0) for rv in (1, 0)]


def split_planes(video, table):
    blocks = [video[:, t * 512 : (t + 1) * 512] for t in range(4)]
    tail = jnp.concatenate([video[:, 2048:2304], jnp.zeros((16, 256), BF16)], axis=1)
    stacked = jnp.concatenate(blocks + [tail], axis=0)
    split = dot(stacked, table)
    out = []
    for plane, offset in enumerate(plane_offsets()):
        parts = [split[t * 16 : (t + 1) * 16, plane * 128 : (plane + 1) * 128] for t in range(5)]
        flat = jnp.concatenate(parts + [jnp.zeros((16, 128), F32)], axis=1)
        out.append(pltpu.roll(flat, offset, 1))
    return out[::-1]


def column_masks():
    row = lax.broadcasted_iota(jnp.int32, (ROWS, POOLED), 0)
    column = lax.broadcasted_iota(jnp.int32, (ROWS, POOLED), 1) % 32
    masks = []
    for shift in range(4):
        at = column + shift - 2 + row % 2
        masks.append((at >= 0) & (at < 32) & (row < 12))
    return masks


def fill_patches(base, patches_ref, k, masks):
    for qu in range(4):
        for qv in range(4):
            shift = qu * 32 + qv
            moved = base if shift == 0 else pltpu.roll(base, BASE_W - shift, 1)
            tile = jnp.where(masks[qv], moved[:, :POOLED], 0.0)
            if shift == 0:
                row = lax.broadcasted_iota(jnp.int32, (ROWS, POOLED), 0)
                tile = jnp.where(row == 12, 1.0, tile)
            at = (qu * 4 + qv) * ROWS
            patches_ref[k, at : at + ROWS, :] = tile.astype(BF16)


def conv_matrix(conv_weight, fold_ref, w2_ref):
    for ab in range(4):
        block = dot(conv_weight, fold_ref[ab][:, :TAPS], NT)
        w2_ref[ab * CH : (ab + 1) * CH, :] = block.astype(BF16)


def remote(src, dst, sends, recvs, send_at, recv_at, peer):
    return pltpu.make_async_remote_copy(
        src_ref=src, dst_ref=dst, send_sem=sends.at[send_at], recv_sem=recvs.at[recv_at],
        device_id=peer, device_id_type=MESH,
    )


def iotas(shape):
    return lax.broadcasted_iota(jnp.int32, shape, 0), lax.broadcasted_iota(jnp.int32, shape, 1)


def one_hot(condition):
    return jnp.where(condition, 1.0, 0.0)


def sorting_matrix(assignment):
    row, _ = iotas((16, 16))
    pick = one_hot(assignment == row)
    row, col = iotas((16, 256))
    wide = dot(pick, one_hot(col % 16 == row))
    row, col = iotas((256, 16))
    tall = dot(one_hot(row // 16 == col), wide)
    row, col = iotas((256, 256))
    return jnp.where(row % 16 == col // 16, tall, 0.0).astype(BF16)


def column(line):
    row, col = iotas((CH, CH))
    one = jnp.sum(jnp.where(row == col, line, 0.0), axis=1, keepdims=True)
    return jnp.concatenate([one] * 4, axis=0)


def block_diagonal(matrix):
    row, col = iotas((CH, 256))
    wide = dot(matrix.astype(BF16), one_hot(col % CH == row).astype(BF16))
    row, col = iotas((256, 256))
    return jnp.where(row // CH == col // CH, jnp.concatenate([wide] * 4, axis=0), 0.0).astype(BF16)


def elu(values):
    return jnp.maximum(values, jnp.exp(jnp.minimum(values, 0.0)) - 1.0)


def finish_small(gmix_ref, gconv_ref, gbias_ref, fold_ref, loss):
    row, col = iotas((256, 256))
    total = jnp.zeros((CH, 256), F32)
    bias = jnp.sum(gbias_ref[...], axis=1, keepdims=True)
    for ab in range(4):
        rows = slice(ab * CH, (ab + 1) * CH)
        place = one_hot((row // CH == ab) & (col == row % CH + TAPS + 1))
        total += dot(gconv_ref[rows, :], fold_ref[ab].astype(F32), precision=lax.Precision.HIGHEST)
        total += dot(gmix_ref[rows, :], place, precision=lax.Precision.HIGHEST)
    line, lane = iotas((CH, 256))
    total = jnp.where(lane == TAPS + 1 + CH, bias, total)
    return jnp.where((lane == TAPS + 2 + CH) & (line == 0), loss, total)


def step_kernel(
    loss_scale,
    count_ref, video_ref, responses_ref, assign_ref, weight_ref, bias1_ref, mix_ref, bias2_ref,
    masks_hbm, featw_hbm, rbias_ref, table_ref, fold_ref,
    small_out, grads_out,
    mask_ref, featw_ref, planes_ref, prev_ref, after_ref, base_ref, w2_ref, mix4_ref, mixt_ref,
    patches_ref, act_ref, feats_ref, psend_ref, precv_ref, tsend_ref, trecv_ref, target_ref,
    turned_ref, proj_ref, mixed_ref, total_ref, loss_ref,
    blocks_ref, got_ref, half_ref, low_ref, up_ref, minus_low_ref, minus_high_ref, plus_low_ref, plus_high_ref, brecv_ref,
    gmix_ref, gconv_ref, gmixb_ref, ar_ref, r1_ref, s2_ref, r2_ref, s3_ref, r3_ref,
    local_sem, halo_s, halo_r, pool_s, pool_r, targ_s, targ_r, pair_s, pair_r, ring_s, ring_r,
    back_s, back_r, a1_s, a1_r, a2_s, a2_r, a3_s, a3_r,
):
    sess = lax.axis_index("sess")
    clip = lax.axis_index("clip")
    row_y = clip // 2
    core = clip % 2

    mask_copy = pltpu.make_async_copy(masks_hbm.at[0], mask_ref, local_sem.at[0])
    featw_copy = pltpu.make_async_copy(featw_hbm.at[0], featw_ref, local_sem.at[1])
    mask_copy.start()
    featw_copy.start()

    def shift(m):
        dz = m % 8 // 2
        return dz, m % 2 * 2 + (dz + m // 8) % 2

    def target_of(m):
        dz, dx = shift(m)
        return (sess // 4 + dz) % 4 * 4 + (sess + dx) % 4

    def source_of(m):
        dz, dx = shift(m)
        return (sess // 4 + 4 - dz) % 4 * 4 + (sess + 4 - dx) % 4

    barrier = pltpu.get_barrier_semaphore()

    def greet_sess(j, carry):
        pl.semaphore_signal(barrier, inc=1, device_id={"sess": (sess + j) % 16}, device_id_type=MESH)
        return carry

    def greet_clip(j, carry):
        pl.semaphore_signal(barrier, inc=1, device_id={"clip": (clip + j) % 8}, device_id_type=MESH)
        return carry

    lax.fori_loop(1, 16, greet_sess, 0)
    lax.fori_loop(1, 8, greet_clip, 0)

    planes = split_planes(video_ref[...], table_ref[...])
    planes_ref[...] = jnp.concatenate(planes, axis=0).astype(BF16)
    sort = sorting_matrix(assign_ref[...])
    stacked = jnp.concatenate([responses_ref[:, q * 256 : (q + 1) * 256] for q in range(16)], axis=0)
    tsend_ref[...] = dot(sort, stacked).astype(BF16).reshape(16, 16, 256)

    conv_matrix(weight_ref[...], fold_ref, w2_ref)
    mix = mix_ref[...].astype(F32)
    mix4_ref[...] = block_diagonal(mix)
    mixt_ref[...] = block_diagonal(mix.T)
    bias1 = column(bias1_ref[...])
    bias2 = column(bias2_ref[...])
    masks = column_masks()

    total_ref[...] = jnp.zeros_like(total_ref)
    loss_ref[...] = jnp.zeros_like(loss_ref)
    gmix_ref[...] = jnp.zeros_like(gmix_ref)
    gconv_ref[...] = jnp.zeros_like(gconv_ref)
    gmixb_ref[...] = jnp.zeros_like(gmixb_ref)
    pl.semaphore_wait(barrier, 22)

    halo_up = remote(planes_ref, prev_ref, halo_s, halo_r, 0, 0, {"sess": (sess + 1) % 16})
    halo_down = remote(planes_ref, after_ref, halo_s, halo_r, 1, 1, {"sess": (sess + 15) % 16})
    halo_up.start()
    halo_down.start()

    def target_copy(m):
        peer = target_of(m)
        return remote(tsend_ref.at[peer], trecv_ref.at[m], targ_s, targ_r, m, m, {"sess": peer})

    def start_target(m, carry):
        target_copy(m).start()
        return carry

    lax.fori_loop(1, 16, start_target, 0)
    trecv_ref[0] = tsend_ref[sess]

    halo_up.wait()
    halo_down.wait()
    none = jnp.zeros((64, BASE_W), BF16)
    prev = jnp.where(sess == 0, none, prev_ref[...])
    after = jnp.where(sess == 15, none, after_ref[...])
    window = jnp.concatenate([prev, planes_ref[...], after], axis=0)
    base_ref[...] = dot(sort[:, :192], window)

    def pooled_copy(m):
        peer = target_of(m)
        return remote(psend_ref.at[peer], precv_ref.at[m], pool_s, pool_r, m, m, {"sess": peer})

    def forward(i, carry):
        steps = [i * GROUP + g for g in range(GROUP)]
        clips = [target_of((j + 1) % 16) for j in steps]
        for k in clips:
            fill_patches(base_ref[pl.ds(pl.multiple_of(k * ROWS, ROWS), ROWS), :], patches_ref, k, masks)
        pre1 = [dot(w2_ref[...], patches_ref[k]) for k in clips]
        act1 = [elu(p + bias1).astype(BF16) for p in pre1]
        pre2 = [dot(mix4_ref[...], a) for a in act1]
        feats = [elu(p + bias2).astype(BF16) for p in pre2]
        for k, a, f in zip(clips, act1, feats):
            act_ref[k] = a
            feats_ref[k] = f
            wide = f.astype(F32)
            total = (wide[0:64] + wide[64:128]) + (wide[128:192] + wide[192:256])
            psend_ref[k] = (total * 0.25).astype(BF16)
        for j in steps:

            @pl.when(j < 15)
            def _():
                pooled_copy(j + 1).start()

        return carry

    lax.fori_loop(0, 16 // GROUP, forward, 0)
    precv_ref[0] = psend_ref[sess]
    mask_copy.wait()
    featw_copy.wait()

    def wait_pooled(m, carry):
        pooled_copy(m).wait()
        return carry

    def wait_target(m, carry):
        target_copy(m).wait()
        return carry

    lax.fori_loop(1, 16, wait_target, 0)
    row, col = iotas((256, 256))
    swap = one_hot((row // 16 == col % 16) & (row % 16 == col // 16)).astype(BF16)
    target_ref[...] = dot(swap, trecv_ref[...].reshape(256, 256))

    partner = {"clip": row_y * 2 + 1 - core}
    right = {"clip": (row_y + 1) % 4 * 2 + core}
    left = {"clip": (row_y + 3) % 4 * 2 + core}
    high = GROWS - LOW

    def pair_copy(t):
        return remote(blocks_ref.at[t], got_ref.at[t], pair_s, pair_r, t, t, partner)

    def ring_copy(src, dst, at, peer):
        return remote(src, dst, ring_s, ring_r, at, at, peer)

    def lows(ref):
        return ref.at[pl.ds(0, LOW)]

    def highs(ref):
        return ref.at[pl.ds(LOW, high)]

    at_two = 4 + (row_y + 2) % 4
    at_one = 4 + (row_y + 1) % 4
    at_three = 4 + (row_y + 3) % 4
    relay_low = ring_copy(lows(half_ref.at[0]), low_ref, 0, right)
    relay_high = ring_copy(highs(half_ref.at[0]), up_ref, 1, left)
    right_high = ring_copy(highs(half_ref.at[1]), minus_high_ref, 2, right)
    left_low = ring_copy(lows(half_ref.at[1]), plus_low_ref, 3, left)
    right_low = ring_copy(lows(blocks_ref.at[at_one]), minus_low_ref, 4, right)
    left_high = ring_copy(highs(blocks_ref.at[at_three]), plus_high_ref, 5, left)

    def readout(t, half):
        parts = (0, 1)
        slots = [t, 4 + t]
        blocks = [t * 2 + 1 - core, t * 2 + core]
        spans = [pl.ds(pl.multiple_of(n * NBLOCK, NBLOCK), NBLOCK) for n in blocks]
        frames = slice(half * HALF, (half + 1) * HALF)
        pooled = precv_ref[frames].reshape(HALF * CH, POOLED)
        for p in parts:
            proj_ref[p] = dot(pooled, mask_ref[:, spans[p]])
        grad_drives = []
        for p in parts:
            n = blocks[p]
            weight = featw_ref[:, spans[p]].astype(F32)
            drives = []
            for f in range(HALF):
                drives.append(jnp.sum(proj_ref[p, f * CH : (f + 1) * CH, :] * weight, axis=0, keepdims=True))
            drive = jnp.concatenate(drives, axis=0) + rbias_ref[:, spans[p]]
            first = target_ref[pl.ds(pl.multiple_of(n * 32 + half * HALF, HALF), HALF), :]
            second = target_ref[pl.ds(pl.multiple_of(n * 32 + 16 + half * HALF, HALF), HALF), :]
            target = jnp.concatenate([first, second], axis=1)
            small = jnp.exp(-jnp.abs(drive))
            rate = jnp.maximum(drive, 0.0) + jnp.log1p(small) + 0.1
            sigmoid = jnp.where(drive >= 0, 1.0, small) / (1.0 + small)
            place = n * NBLOCK + lax.broadcasted_iota(jnp.int32, (HALF, NBLOCK), 1)
            alive = place < count_ref[0]
            terms = jnp.where(alive, rate - target * jnp.log(rate), 0.0)
            loss_ref[...] += jnp.sum(terms, keepdims=True) * loss_scale
            grad_drives.append(jnp.where(alive, (1.0 - target / rate) * sigmoid, 0.0) * loss_scale)
            for f in range(HALF):
                mixed_ref[p, f * CH : (f + 1) * CH, :] = (grad_drives[p][f : f + 1, :] * weight).astype(BF16)
        mask_grads = [dot(turned_ref[...], mixed_ref[p]) for p in parts]
        total_ref[...] += sum(dot(mixed_ref[p], mask_ref[:, spans[p]], NT) for p in parts)
        for p in parts:
            slot = slots[p]
            feat = jnp.zeros((CH, NBLOCK), F32)
            for f in range(HALF):
                feat += grad_drives[p][f : f + 1, :] * proj_ref[p, f * CH : (f + 1) * CH, :]
            bias_grad = jnp.sum(grad_drives[p], axis=0, keepdims=True)
            bias_grad = jnp.broadcast_to(bias_grad, (GROWS - POOLED - CH, NBLOCK))
            if half == 0:
                blocks_ref[slot, 0:POOLED, :] = mask_grads[p]
                blocks_ref[slot, POOLED : POOLED + CH, :] = feat
                blocks_ref[slot, POOLED + CH : GROWS, :] = bias_grad
            else:
                blocks_ref[slot, 0:POOLED, :] += mask_grads[p]
                blocks_ref[slot, POOLED : POOLED + CH, :] += feat
                blocks_ref[slot, POOLED + CH : GROWS, :] += bias_grad

    def back_copy(m):
        peer = source_of(m)
        return remote(psend_ref.at[m], brecv_ref.at[m], back_s, back_r, m, m, {"sess": peer})

    def send_back(m, carry):
        psend_ref[m] = total_ref[pl.ds(pl.multiple_of(m % HALF * CH, CH), CH), :].astype(BF16)

        @pl.when(m > 0)
        def _():
            back_copy(m).start()

        return carry

    def first_pass(t, carry):
        readout(t, 0)
        return carry

    lax.fori_loop(1, HALF, wait_pooled, 0)
    turned_ref[...] = precv_ref[0:HALF].reshape(HALF * CH, POOLED).T
    lax.fori_loop(0, 4, first_pass, 0)
    lax.fori_loop(HALF, 16, wait_pooled, 0)
    lax.fori_loop(0, HALF, send_back, 0)
    total_ref[...] = jnp.zeros_like(total_ref)
    brecv_ref[0] = psend_ref[0]
    turned_ref[...] = precv_ref[HALF:16].reshape(HALF * CH, POOLED).T

    def turn_of(i):
        return (row_y + jnp.where(i == 0, 2, jnp.where(i == 1, 1, jnp.where(i == 2, 3, 0)))) % 4

    def take_pair(t):
        pair_copy(t).wait()
        blocks_ref[4 + t] += got_ref[t]

    def phase(i, carry):
        t = turn_of(i)
        readout(t, 1)
        pair_copy(t).start()

        @pl.when(i > 0)
        def _():
            take_pair(turn_of(i - 1))

        @pl.when(i == 1)
        def _():
            half_ref[0] = blocks_ref[at_two].astype(BF16)
            relay_low.start()
            relay_high.start()

        @pl.when(i == 2)
        def _():
            half_ref[1, LOW:GROWS, :] = blocks_ref[at_one, LOW:GROWS, :].astype(BF16)
            right_high.start()

        @pl.when(i == 3)
        def _():
            half_ref[1, 0:LOW, :] = blocks_ref[at_three, 0:LOW, :].astype(BF16)
            left_low.start()

        return carry

    lax.fori_loop(0, 4, phase, 0)
    lax.fori_loop(HALF, 16, send_back, 0)

    one_half = jnp.asarray(1.0, BF16)
    zero_half = jnp.asarray(0.0, BF16)

    def backward(i, carry):
        steps = [i * GROUP + g for g in range(GROUP)]
        clips = [target_of(m) for m in steps]

        @pl.when(i == RELAY_AT)
        def _():
            relay_low.wait()
            blocks_ref[at_one, 0:LOW, :] += low_ref[...].astype(F32)
            right_low.start()
            relay_high.wait()
            blocks_ref[at_three, LOW:GROWS, :] += up_ref[...].astype(F32)
            left_high.start()

        for m in steps:

            @pl.when(m > 0)
            def _():
                back_copy(m).wait()

        grads = [brecv_ref[m] * jnp.asarray(0.25, BF16) for m in steps]
        slopes = [one_half + jnp.minimum(feats_ref[k], zero_half) for k in clips]
        pre2_grad = [jnp.concatenate([g] * 4, axis=0) * s for g, s in zip(grads, slopes)]
        act1 = [act_ref[k] for k in clips]
        act1_grad = [dot(mixt_ref[...], p) for p in pre2_grad]
        gmix_ref[...] += sum(dot(p, a, NT) for p, a in zip(pre2_grad, act1))
        slopes = [(one_half + jnp.minimum(a, zero_half)).astype(F32) for a in act1]
        pre1_grad = [(g * s).astype(BF16) for g, s in zip(act1_grad, slopes)]
        wide = sum(p.astype(F32) for p in pre2_grad)
        gmixb_ref[...] += (wide[0:64] + wide[64:128]) + (wide[128:192] + wide[192:256])
        gconv_ref[...] += sum(dot(p, patches_ref[k], NT) for p, k in zip(pre1_grad, clips))
        return carry

    lax.fori_loop(0, 16 // GROUP, backward, 0)

    small = finish_small(gmix_ref, gconv_ref, gmixb_ref, fold_ref, loss_ref[...])
    for piece in range(16):
        top, lane = piece // 2 * 8, piece % 2 * 128
        ar_ref[piece] = small[top : top + 8, lane : lane + 128]

    def a1_copy(j, here):
        peer = (sess + 1 + j) % 16
        return remote(ar_ref.at[peer], r1_ref.at[here], a1_s, a1_r, peer, here, {"sess": peer})

    def a2_copy(j, here):
        peer = (clip + 1 + j) % 8
        return remote(s2_ref, r2_ref.at[here], a2_s, a2_r, peer, here, {"clip": peer})

    def a3_copy(j, here):
        peer = (sess + 1 + j) % 16
        return remote(s3_ref, r3_ref.at[here], a3_s, a3_r, peer, here, {"sess": peer})

    def begin_all(copy, count, mine):
        def begin(j, carry):
            copy(j, mine).start()
            return carry

        lax.fori_loop(0, count, begin, 0)

    def finish_all(copy, count, mine):
        def finish(j, carry):
            copy(j, (mine + count - j) % (count + 1)).wait()
            return carry

        lax.fori_loop(0, count, finish, 0)

    begin_all(a1_copy, 15, sess)
    r1_ref[sess] = ar_ref[sess]
    finish_all(a1_copy, 15, sess)
    part = jnp.sum(r1_ref[...], axis=0)
    s2_ref[...] = part
    begin_all(a2_copy, 7, clip)
    r2_ref[clip] = part
    finish_all(a2_copy, 7, clip)
    part = jnp.sum(r2_ref[...], axis=0)
    s3_ref[...] = part
    begin_all(a3_copy, 15, sess)
    r3_ref[sess] = part
    take_pair(row_y)
    right_high.wait()
    left_low.wait()
    right_low.wait()
    left_high.wait()
    low = blocks_ref[4 + row_y, 0:LOW, :] + minus_low_ref[...]
    grads_out[0:LOW, :] = low + plus_low_ref[...].astype(F32)
    top = blocks_ref[4 + row_y, LOW:GROWS, :] + plus_high_ref[...]
    grads_out[LOW:GROWS, :] = top + minus_high_ref[...].astype(F32)
    finish_all(a3_copy, 15, sess)
    lines = [jnp.concatenate([r3_ref[2 * r], r3_ref[2 * r + 1]], axis=1) for r in range(8)]
    small_out[...] = jnp.concatenate(lines, axis=0)


def split_kernel(
    small_ref, grads_ref, loss_out, conv_out, convb_out, mix_out, mixb_out, gmask_out, gfeat_out, gbias_out
):
    small = small_ref[...]
    conv_out[...] = small[:, :TAPS]
    row, col = iotas((CH, CH))
    convb_out[...] = jnp.sum(jnp.where(row == col, small[:, TAPS : TAPS + 1], 0.0), axis=0, keepdims=True)
    mix_out[...] = small[:, TAPS + 1 : TAPS + 1 + CH]
    mixb = small[:, TAPS + 1 + CH : TAPS + 2 + CH]
    mixb_out[...] = jnp.sum(jnp.where(row == col, mixb, 0.0), axis=0, keepdims=True)
    loss_out[...] = small[0:1, TAPS + 2 + CH : TAPS + 3 + CH]
    gmask_out[...] = grads_ref[0:POOLED]
    gfeat_out[...] = grads_ref[POOLED : POOLED + CH]
    gbias_out[...] = grads_ref[POOLED + CH : POOLED + CH + 1]


def run_split(small, grads):
    outs = [(1, 1), (CH, TAPS), (1, CH), (CH, CH), (1, CH), (POOLED, NBLOCK), (CH, NBLOCK), (1, NBLOCK)]
    return pl.pallas_call(
        split_kernel,
        out_shape=[jax.ShapeDtypeStruct(shape, F32) for shape in outs],
        name="split_results",
    )(small, grads)


def run_step(loss_scale, *args):
    def vmem(shape, dtype):
        return pltpu.VMEM(shape, dtype)

    def dma(n):
        return pltpu.SemaphoreType.DMA((n,))

    whole = pl.BlockSpec(memory_space=pltpu.VMEM)
    anywhere = pl.BlockSpec(memory_space=pl.ANY)
    smem = pl.BlockSpec(memory_space=pltpu.SMEM)
    outs = [(CH, 256), (GROWS, NBLOCK)]
    neurons = args[8].shape[2]
    return pl.pallas_call(
        functools.partial(step_kernel, loss_scale),
        in_specs=[smem] + [whole] * 7 + [anywhere] * 2 + [whole] * 3,
        out_specs=[whole] * 2,
        out_shape=[jax.ShapeDtypeStruct(shape, F32) for shape in outs],
        scratch_shapes=[
            vmem((POOLED, neurons), BF16),
            vmem((CH, neurons), BF16),
            vmem((64, BASE_W), BF16),
            vmem((64, BASE_W), BF16),
            vmem((64, BASE_W), BF16),
            vmem((256, BASE_W), F32),
            vmem((256, 256), BF16),
            vmem((256, 256), BF16),
            vmem((256, 256), BF16),
            vmem((16, 256, POOLED), BF16),
            vmem((16, 256, POOLED), BF16),
            vmem((16, 256, POOLED), BF16),
            vmem((16, CH, POOLED), BF16),
            vmem((16, CH, POOLED), BF16),
            vmem((16, 16, 256), BF16),
            vmem((16, 16, 256), BF16),
            vmem((256, 256), F32),
            vmem((POOLED, HALF * CH), BF16),
            vmem((2, HALF * CH, NBLOCK), F32),
            vmem((2, HALF * CH, NBLOCK), BF16),
            vmem((HALF * CH, POOLED), F32),
            vmem((1, 1), F32),
            vmem((8, GROWS, NBLOCK), F32),
            vmem((4, GROWS, NBLOCK), F32),
            vmem((2, GROWS, NBLOCK), BF16),
            vmem((LOW, NBLOCK), BF16),
            vmem((GROWS - LOW, NBLOCK), BF16),
            vmem((LOW, NBLOCK), F32),
            vmem((GROWS - LOW, NBLOCK), BF16),
            vmem((LOW, NBLOCK), BF16),
            vmem((GROWS - LOW, NBLOCK), F32),
            vmem((16, CH, POOLED), BF16),
            vmem((256, 256), F32),
            vmem((256, 256), F32),
            vmem((CH, POOLED), F32),
            vmem((16, 8, 128), F32),
            vmem((16, 8, 128), F32),
            vmem((8, 128), F32),
            vmem((8, 8, 128), F32),
            vmem((8, 128), F32),
            vmem((16, 8, 128), F32),
        ]
        + [dma(n) for n in (2, 2, 2, 16, 16, 16, 16, 4, 4, 6, 6, 16, 16, 16, 16, 8, 8, 16, 16)],
        compiler_params=pltpu.CompilerParams(
            collective_id=0, has_side_effects=True, vmem_limit_bytes=VM
        ),
        name="train_step",
    )(*args)


def per_device(
    video, responses, assignment, counts, conv_weight, conv_bias, mix_weight, mix_bias, masks, feat_w, readout_bias,
):
    sess_total = lax.axis_size("sess")
    clip_total = lax.axis_size("clip")
    loss_scale = 1.0 / (video.shape[0] * clip_total * sess_total)
    small, grads = run_step(
        loss_scale,
        counts,
        video.reshape(video.shape[0], -1),
        responses.reshape(responses.shape[0], -1),
        assignment[None],
        conv_weight,
        conv_bias[None],
        mix_weight,
        mix_bias[None],
        jnp.swapaxes(masks, 1, 2),
        jnp.swapaxes(feat_w, 1, 2),
        readout_bias,
        jnp.asarray(split_table(), BF16),
        jnp.asarray(tap_tables(), BF16),
    )
    loss, gconv, gconvb, gmix, gmixb, gmask, gfeat, gbias = run_split(small, grads)
    return (
        loss[0, 0],
        gconv,
        gconvb[0],
        gmix,
        gmixb[0],
        gmask.T[None],
        gfeat.T[None],
        gbias,
    )


def solution(mesh):
    return jax.shard_map(
        per_device,
        mesh=mesh,
        in_specs=(
            P("clip", "sess", None),
            P("clip", "sess", None),
            P("clip"),
            P("sess"),
            P(),
            P(),
            P(),
            P(),
            P("sess", None, None),
            P("sess", None, None),
            P("sess", None),
        ),
        out_specs=(
            P(),
            P(),
            P(),
            P(),
            P(),
            P("sess", "clip", None),
            P("sess", "clip", None),
            P("sess", "clip"),
        ),
        check_vma=False,
    )
```
